512 devices in a mesh: rows: 8 (over x_lo, y), cols: 64 (over z, x_hi, core).
Axes of the slice: x: 4 (x_hi: 2, x_lo: 2; x = x_hi * 2 + x_lo), y: 4, z: 16, core: 2. Of those that a mesh axis runs over, the one named last changes fastest.
Arguments:
- fronts: bfloat16 [8, 128, 16, 8192], P('rows', None, None, 'cols')
- factors: bfloat16 [8, 2048, 8192], P('rows', None, 'cols'), may hold values from -0.125 to 0.125
- site_tensors: float32 [8, 16, 4096], P('rows', None, 'cols'), may hold values from -6 to 6
- operators: float32 [8, 4, 256], P('rows', None, 'cols'), may hold values from -6 to 6
- kept_ranks: int32 [8, 64], P('rows', 'cols'), may hold values from 64 to 128, as said below
Outputs:
- next_fronts: bfloat16 [8, 128, 16, 8192], P('rows', None, None, 'cols')
The draws below stay inside these ranges and needn't reach their ends.
Inputs may be any that keep to these rules, and one draw needn't show every extreme that they name: `kept_ranks`: each bond's kept rank is a multiple of 8; in every draw some bond keeps all 128.
All inputs are finite; a program needn't handle non-finite values. Where the reference program divides by a largest or mean magnitude, that divisor is 1e-20 or more.
Results may differ from the reference program's by a relative error of at most 0.03.
Values may be sent and summed in bfloat16 or wider, within the bound.
A program may use at most 64 MiB of HBM per device.

```python
import math
import jax
import jax.numpy as jnp
from jax import lax

X = 128
D = 4
S = 4
D2 = 16
NR = 8
NC = 64


def draw_fronts(key, part):
    key = jax.random.fold_in(key, 11)
    base_key, column_key, row_key = jax.random.split(key, 3)
    full_shape = (NR, X, D2, NC * X)
    column_scale = jnp.exp(jax.random.uniform(column_key, (NR, 1, 1, NC), jnp.float32) * math.log(10.0))
    row_scale = jnp.exp(jax.random.uniform(row_key, (NR, X, 1, 1), jnp.float32) * math.log(4.0))
    values = jax.random.normal(base_key, full_shape, jnp.float32)
    column_scale = jnp.repeat(column_scale, X, axis=3)
    return (values * column_scale * row_scale * 0.25).astype(jnp.bfloat16)


def draw_kept_ranks(key, part):
    key = jax.random.fold_in(key, 23)
    step_key, spot_key = jax.random.split(key)
    multiples = jax.random.randint(step_key, (NR * NC,), X // 16, X // 8 + 1)
    chosen = jax.random.randint(spot_key, (), 0, NR * NC)
    filled = jnp.where(jnp.arange(NR * NC) == chosen, X // 8, multiples)
    return (filled * 8).reshape(NR, NC).astype(jnp.int32)


def steps_of(stream_key, dims, pieces, least, high):
    gain, own = 1.0, jax.random.fold_in(stream_key, 6)
    for position, blocks in pieces:
        heights = jnp.exp(jax.random.uniform(jax.random.fold_in(own, position), (blocks,), jnp.float32, least / len(pieces), high / len(pieces)))
        gain = gain * jnp.repeat(heights, dims[position] // blocks).reshape([-1 if axis == position else 1 for axis in range(len(dims))])
    return gain


def bell_draw(stream_key, shape, scale, most, shards=(), kind=jnp.bfloat16):
    result = jax.random.normal(stream_key, shape, jnp.float32) * scale
    if len(shards) > 0:
        result = steps_of(stream_key, shape, shards, -0.22, 0.18) * result
    return jnp.clip(result, min=-most, max=most).astype(kind)


def setup_inputs(seed: int = 0) -> dict:
    keys = jax.random.split(jax.random.key(seed), 6)
    fronts = draw_fronts(jax.random.fold_in(keys[5], 71), 0)
    factors = bell_draw(keys[1], (NR, X * D2, NC * X), (X * D2) ** -0.5, 0.125, ((0, 8), (2, 64)))
    site_tensors = bell_draw(keys[2], (NR, D * D, NC * D * D * S), 1.0, 6.0, ((0, 8), (2, 64)), jnp.float32)
    operators = bell_draw(keys[3], (NR, S, NC * S), 1.0, 6.0, ((0, 8), (2, 64)), jnp.float32)
    kept_ranks = draw_kept_ranks(jax.random.fold_in(keys[5], 71), 0)
    return {"fronts": fronts, "factors": factors, "site_tensors": site_tensors, "operators": operators, "kept_ranks": kept_ranks}


epsilon = 1e-6


def double_layer(tensor, operator):
    return jnp.einsum('vlwqs,st,VLWQt->lLvVwWqQ', tensor, operator, tensor)


def absorb(packed):
    own_front, left_factor, right_factor, doubled = packed
    double_width = D * D
    left_view = left_factor.reshape(X, double_width, X).astype(jnp.float32)
    projected = jnp.einsum('xla,xvy->lavy', left_view, own_front.astype(jnp.float32)).astype(jnp.bfloat16)
    absorbed = jnp.einsum('lavy,lvwq->awqy', projected.astype(jnp.float32), doubled.astype(jnp.float32)).astype(jnp.bfloat16)
    right_view = right_factor.reshape(X, double_width, X).astype(jnp.float32)
    return jnp.einsum('awqy,yqb->awb', absorbed.astype(jnp.float32), right_view).astype(jnp.bfloat16)


def reference(fronts, factors, site_tensors, operators, kept_ranks):
    double_width = D * D
    results = []
    for row_group in range(NR):
        tensors = site_tensors[row_group].reshape(D, D, NC, D, D, S).transpose(2, 0, 1, 3, 4, 5)
        if row_group % 2 == 1:
            tensors = tensors.transpose(0, 3, 2, 1, 4, 5)
        column_ops = operators[row_group].reshape(S, NC, S).transpose(1, 0, 2)
        doubled = jax.vmap(double_layer)(tensors, column_ops)
        doubled = doubled.reshape(NC, double_width, double_width, double_width, double_width).astype(jnp.bfloat16)
        factor_blocks = factors[row_group].reshape(X * double_width, NC, X).transpose(1, 0, 2)
        columns = jnp.arange(X, dtype=jnp.int32)
        masked = jnp.where(columns[None, None, :] < kept_ranks[row_group][:, None, None], factor_blocks, jnp.zeros_like(factor_blocks))
        left_factors = jnp.roll(masked, 1, axis=0)
        column_fronts = fronts[row_group].reshape(X, double_width, NC, X).transpose(2, 0, 1, 3)
        unscaled = lax.map(absorb, (column_fronts, left_factors, masked, doubled))
        unscaled = lax.optimization_barrier(unscaled)
        widened = unscaled.astype(jnp.float32)
        row_top = jnp.max(jnp.abs(widened))
        normalized = (widened / (row_top + epsilon)).astype(jnp.bfloat16)
        results.append(normalized.transpose(1, 2, 0, 3).reshape(X, double_width, NC * X))
    ordered = [results[row_group ^ 1] for row_group in range(NR)]
    return jnp.stack(ordered)
```

```python
import jax
import jax.numpy as jnp
from jax import lax
from jax.experimental import pallas as pl
from jax.experimental.pallas import tpu as pltpu
from jax.sharding import PartitionSpec as P

X = 128
D = 4
S = 4
D2 = D * D
TILE = D2 * D2
CHUNKS = X // D2
QUAD = 4
EPSILON = 1e-06

MESH = pl.DeviceIdType.MESH
BF16 = jnp.bfloat16
F32 = jnp.float32
NT = (((1,), (1,)), ((), ()))


def dot(a, b):
    return jnp.dot(a, b, preferred_element_type=F32)


def dot_nt(a, b):
    return lax.dot_general(a, b, NT, preferred_element_type=F32)


def iota(shape, dim):
    return lax.broadcasted_iota(jnp.int32, shape, dim)


def select(condition):
    return jnp.where(condition, 1.0, 0.0).astype(BF16)


def swap_16():
    rows, columns = iota((TILE, TILE), 0), iota((TILE, TILE), 1)
    return select(columns == (rows % D2) * D2 + rows // D2)


def double_layer(site, operators, odd):
    wide = jnp.concatenate([site, site], axis=1)
    rows, columns = iota(wide.shape, 0), iota(wide.shape, 1)
    shift = (rows // D - columns // D2 + 2 * D) % D
    swapped = jnp.where(shift == 0, wide, 0.0)
    for k in range(1, D):
        moved = pltpu.roll(pltpu.roll(wide, D * k, 0), wide.shape[1] - D2 * k, 1)
        swapped = jnp.where(shift == k, moved, swapped)
    wide = jnp.where(odd == 1, swapped, wide)
    half = D * D2
    high = wide.astype(BF16)
    low = (wide - high.astype(F32)).astype(BF16)
    parts = jnp.where(columns < half, high.astype(F32), low.astype(F32)).astype(BF16)
    index, entry = iota((TILE, D2), 0), iota((TILE, D2), 1)
    v_index, l_index = index // D2, index % D2
    ket_rows = select(entry == (v_index // D) * D + l_index // D)
    bra_rows = select(entry == (v_index % D) * D + l_index % D)
    ket = dot(ket_rows, parts).astype(BF16)
    bra = dot(bra_rows, parts).astype(BF16)
    index, entry = iota((TILE, 4 * half), 0), iota((TILE, 4 * half), 1)
    q_index, w_index = index // D2, index % D2
    ket_place = (w_index // D) * D2 + (q_index // D) * S
    bra_place = (w_index % D) * D2 + (q_index % D) * S
    ket_match = entry % half - entry % S == ket_place
    ket = jnp.concatenate([ket, ket], axis=1)
    lanes = iota((8, 4 * half), 1)
    total = None
    for t in range(S):
        column = jnp.zeros(lanes.shape, F32)
        for s in range(S):
            column = jnp.where(lanes % S == s, operators[s][t], column)
        high = column.astype(BF16).astype(F32)
        column = jnp.where(lanes < 2 * half, high, column - high)[:1]
        left = dot_nt(jnp.where(ket_match, column, 0.0).astype(BF16), ket)
        places = entry[:, : 2 * half] % half == bra_place[:, : 2 * half] + t
        term = left * dot_nt(select(places), bra)
        total = term if total is None else total + term
    return total.astype(BF16)


def kernel(
    n_columns,
    kept_ref,
    operator_hbm,
    site_hbm,
    front_hbm,
    factor_hbm,
    arrived_ref,
    divisor_ref,
    operator_ref,
    site_ref,
    front_ref,
    factor_ref,
    planes_ref,
    turned_ref,
    sent_ref,
    left_ref,
    front_planes_ref,
    doubled_ref,
    projected_a,
    projected_b,
    absorbed_a,
    absorbed_b,
    unscaled_ref,
    quad_ref,
    ring_ref,
    load_sem,
    left_send,
    left_recv,
    front_send,
    front_recv,
    quad_send,
    quad_recv,
    ring_send,
    ring_recv,
    top_send,
    top_recv,
):
    n_ring = n_columns // QUAD
    row, column = lax.axis_index("rows"), lax.axis_index("cols")
    odd = lax.rem(row, 2)
    partner = row + 1 - 2 * odd
    before = lax.rem(column + n_columns - 1, n_columns)
    behind = lax.rem(column + 1, n_columns)
    place, member = column // QUAD, lax.rem(column, QUAD)

    def load(source, target, k):
        copy = pltpu.make_async_copy(source, target, load_sem.at[k])
        copy.start()
        return copy

    load_factor = load(factor_hbm, factor_ref, 0)
    load_front = load(front_hbm, front_ref, 1)
    load_site = load(site_hbm, site_ref, 2)
    load_operator = load(operator_hbm, operator_ref, 3)

    barrier = pltpu.get_barrier_semaphore()

    def greet(to_row, to_column):
        pl.semaphore_signal(barrier, inc=1, device_id=(to_row, to_column), device_id_type=MESH)

    def quad_column(k):
        return place * QUAD + lax.rem(member + k, QUAD)

    def ring_column(k):
        return lax.rem(place + k, n_ring) * QUAD + member

    greet(row, before)
    greet(row, behind)
    greet(partner, column)
    for k in range(1, QUAD):
        greet(row, quad_column(k))

    def greet_ring(k, carry):
        greet(row, ring_column(k))
        return carry

    lax.fori_loop(1, n_ring, greet_ring, 0)

    def chunk(ref, i):
        return ref.at[pl.ds(pl.multiple_of(i * TILE, TILE), TILE), :]

    def beside(ref, i):
        return jnp.concatenate(
            [ref[i * TILE : (i + 1) * TILE, :], ref[(i + 1) * TILE : (i + 2) * TILE, :]], axis=1
        )

    swap = swap_16()
    identity = select(iota((X, X), 0) == iota((X, X), 1))
    kept_columns = iota((TILE, 2 * X), 1) % X < kept_ref[0, 0]
    load_factor.wait()

    for i in range(0, CHUNKS, 2):
        both = jnp.where(kept_columns, dot(swap, beside(factor_ref, i)), 0.0).astype(BF16)
        for k in range(2):
            for q in range(D2):
                start = q * X + (i + k) * D2
                planes_ref[start : start + D2, :] = both[
                    q * D2 : (q + 1) * D2, k * X : (k + 1) * X
                ]

    for q in range(0, D2, 2):
        both = dot_nt(identity, planes_ref[q * X : (q + 2) * X, :]).astype(BF16)
        for k in range(2):
            for i in range(CHUNKS):
                start = i * TILE + (q + k) * D2
                turned_ref[start : start + D2, :] = both[
                    i * D2 : (i + 1) * D2, k * X : (k + 1) * X
                ]

    for i in range(0, CHUNKS, 2):
        both = dot(swap, beside(turned_ref, i)).astype(BF16)
        for k in range(2):
            sent_ref[(i + k) * TILE : (i + k + 1) * TILE, :] = both[:, k * X : (k + 1) * X]

    pl.semaphore_wait(barrier, 2 + 1 + (QUAD - 1) + (n_ring - 1))

    def left_copy(i):
        return pltpu.make_async_remote_copy(
            src_ref=chunk(sent_ref, i),
            dst_ref=chunk(left_ref, i),
            send_sem=left_send.at[i],
            recv_sem=left_recv.at[i],
            device_id=(row, behind),
            device_id_type=MESH,
        )

    def start_left(i, carry):
        left_copy(i).start()
        return carry

    lax.fori_loop(0, CHUNKS, start_left, 0)

    load_front.wait()
    for i in range(0, CHUNKS, 2):
        both = dot(swap, beside(front_ref, i)).astype(BF16)
        for k in range(2):
            for v in range(D2):
                front_planes_ref[(i + k) * D2 : (i + k + 1) * D2, v * X : (v + 1) * X] = both[
                    v * D2 : (v + 1) * D2, k * X : (k + 1) * X
                ]

    load_site.wait()
    load_operator.wait()
    doubled_ref[...] = double_layer(
        site_ref[0], [[operator_ref[0, s, t] for t in range(S)] for s in range(S)], odd
    )

    def front_copy(i):
        return pltpu.make_async_remote_copy(
            src_ref=chunk(unscaled_ref, i),
            dst_ref=chunk(arrived_ref, i),
            send_sem=front_send.at[i],
            recv_sem=front_recv.at[i],
            device_id=(partner, column),
            device_id_type=MESH,
        )

    def finish_chunk(absorbed_ref, i, top):
        result = dot(absorbed_ref[...], planes_ref[...])
        unscaled_ref[pl.ds(pl.multiple_of(i * TILE, TILE), TILE), :] = result.astype(BF16)
        front_copy(i).start()
        return jnp.maximum(top, jnp.max(jnp.abs(result).reshape(TILE // 8, 8, X), axis=0))

    def project(left, projected_ref, v):
        both = dot(left, front_planes_ref[:, v * X : (v + 2) * X]).astype(BF16)
        for k in range(2):
            projected_ref[:, (v + k) * D2 : (v + k + 1) * D2, :] = both[
                :, k * X : (k + 1) * X
            ].reshape(D2, D2, X)

    def absorb(projected_ref, absorbed_ref, a):
        pair = jnp.concatenate([projected_ref[a], projected_ref[a + 1]], axis=1)
        both = dot(doubled_ref[...], pair).astype(BF16)
        for k in range(2):
            for q in range(D2):
                absorbed_ref[(a + k) * D2 : (a + k + 1) * D2, q * X : (q + 1) * X] = both[
                    q * D2 : (q + 1) * D2, k * X : (k + 1) * X
                ]

    def step(i, even, top, first=True, middle=True, last=True):
        projected = (projected_a, projected_b) if even else (projected_b, projected_a)
        absorbed = (absorbed_a, absorbed_b) if even else (absorbed_b, absorbed_a)
        if last:
            top = finish_chunk(absorbed[1], i - 1, top)
        if first:
            left_copy(i + 1).wait_recv()
            left = left_ref[pl.ds(pl.multiple_of((i + 1) * TILE, TILE), TILE), :]
        for k in range(0, D2, 2):
            if first:
                project(left, projected[1], k)
            if middle:
                absorb(projected[0], absorbed[0], k)
        return top

    def two_steps(n, top):
        return step(2 * n + 2, True, step(2 * n + 1, False, top))

    top = jnp.zeros((8, X), F32)
    step(-1, False, top, middle=False, last=False)
    step(0, True, top, last=False)
    top = lax.fori_loop(0, (CHUNKS - 2) // 2, two_steps, top)
    top = step(CHUNKS - 1, False, top, first=False)
    top = step(CHUNKS, True, top, first=False, middle=False)
    top = top.astype(BF16).astype(F32)

    def quad_copy(k):
        return pltpu.make_async_remote_copy(
            src_ref=quad_ref.at[member],
            dst_ref=quad_ref.at[member],
            send_sem=quad_send.at[k],
            recv_sem=quad_recv.at[member],
            device_id=(row, quad_column(k)),
            device_id_type=MESH,
        )

    def arrival(ref, sems, slot):
        return pltpu.make_async_remote_copy(
            src_ref=ref.at[slot],
            dst_ref=ref.at[slot],
            send_sem=sems.at[slot],
            recv_sem=sems.at[slot],
            device_id=(row, behind),
            device_id_type=MESH,
        )

    quad_ref[member] = top
    for k in range(1, QUAD):
        quad_copy(k).start()
    for k in range(1, QUAD):
        arrival(quad_ref, quad_recv, lax.rem(member + k, QUAD)).wait_recv()
    for k in range(1, QUAD):
        quad_copy(k).wait_send()
    ring_ref[place] = jnp.max(quad_ref[:QUAD], axis=0)

    def ring_copy(k):
        return pltpu.make_async_remote_copy(
            src_ref=ring_ref.at[place],
            dst_ref=ring_ref.at[place],
            send_sem=ring_send.at[k],
            recv_sem=ring_recv.at[place],
            device_id=(row, ring_column(k)),
            device_id_type=MESH,
        )

    def start_ring(k, carry):
        ring_copy(k).start()
        return carry

    def end_ring(k, carry):
        arrival(ring_ref, ring_recv, lax.rem(place + k, n_ring)).wait_recv()
        ring_copy(k).wait_send()
        return carry

    lax.fori_loop(1, n_ring, start_ring, 0)
    lax.fori_loop(1, n_ring, end_ring, 0)

    own_top = quad_ref.at[QUAD]
    own_top[...] = jnp.broadcast_to(jnp.max(ring_ref[...]), (8, X))
    top_copy = pltpu.make_async_remote_copy(
        src_ref=own_top,
        dst_ref=quad_ref.at[QUAD + 1],
        send_sem=top_send,
        recv_sem=top_recv,
        device_id=(partner, column),
        device_id_type=MESH,
    )
    top_copy.start()
    top_copy.wait_recv()
    divisor_ref[...] = quad_ref[QUAD + 1, :1, :1] + EPSILON

    def finish(i, carry):
        left_copy(i).wait_send()
        front_copy(i).wait()
        return carry

    lax.fori_loop(0, CHUNKS, finish, 0)
    top_copy.wait_send()


def per_device(fronts, factors, site_tensors, operators, kept_ranks):
    n_columns = lax.axis_size("cols")
    rows = X * D2
    smem = pl.BlockSpec(memory_space=pltpu.SMEM)
    hbm = pl.BlockSpec(memory_space=pltpu.HBM)
    vmem = pl.BlockSpec(memory_space=pltpu.VMEM)
    anywhere = pl.BlockSpec(memory_space=pl.ANY)
    dma = pltpu.SemaphoreType.DMA

    def body(*refs):
        kernel(n_columns, *refs)

    flops = 2 * 4 * X * X * X * D2 * D2
    arrived, divisor = pl.pallas_call(
        body,
        out_shape=(
            jax.ShapeDtypeStruct((rows, X), BF16),
            jax.ShapeDtypeStruct((1, 1), F32),
        ),
        in_specs=[smem] + [hbm] * 4,
        out_specs=(anywhere, vmem),
        scratch_shapes=[
            pltpu.SMEM(operators.shape, F32),
            pltpu.VMEM(site_tensors.shape, F32),
            pltpu.VMEM((rows, X), BF16),
            pltpu.VMEM((rows, X), BF16),
            pltpu.VMEM((rows, X), BF16),
            pltpu.VMEM((rows, X), BF16),
            pltpu.VMEM((rows, X), BF16),
            pltpu.VMEM((rows, X), BF16),
            pltpu.VMEM((X, rows), BF16),
            pltpu.VMEM((TILE, TILE), BF16),
            pltpu.VMEM((D2, TILE, X), BF16),
            pltpu.VMEM((D2, TILE, X), BF16),
            pltpu.VMEM((TILE, rows), BF16),
            pltpu.VMEM((TILE, rows), BF16),
            pltpu.VMEM((rows, X), BF16),
            pltpu.VMEM((QUAD + 2, 8, X), F32),
            pltpu.VMEM((n_columns // QUAD, 8, X), F32),
            dma((4,)),
            dma((CHUNKS,)),
            dma((CHUNKS,)),
            dma((CHUNKS,)),
            dma((CHUNKS,)),
            dma((QUAD,)),
            dma((QUAD,)),
            dma((n_columns // QUAD,)),
            dma((n_columns // QUAD,)),
            dma,
            dma,
        ],
        compiler_params=pltpu.CompilerParams(
            collective_id=0, has_side_effects=True, vmem_limit_bytes=40 * 2**20
        ),
        cost_estimate=pl.CostEstimate(flops=flops, bytes_accessed=3 * 2**19, transcendentals=0),
    )(
        kept_ranks,
        *(
            pltpu.with_memory_space_constraint(operand, pltpu.HBM)
            for operand in (
                operators,
                site_tensors,
                fronts.reshape(rows, X),
                factors.reshape(rows, X),
            )
        )
    )
    normalized = arrived.astype(F32) / divisor[0, 0]
    return normalized.astype(BF16).reshape(1, X, D2, X)


def solution(mesh):
    return jax.shard_map(
        per_device,
        mesh=mesh,
        in_specs=(
            P("rows", None, None, "cols"),
            P("rows", None, "cols"),
            P("rows", None, "cols"),
            P("rows", None, "cols"),
            P("rows", "cols"),
        ),
        out_specs=P("rows", None, None, "cols"),
        check_vma=False,
    )
```

```python
import jax
import jax.numpy as jnp
from jax import lax
from jax.experimental import pallas as pl
from jax.experimental.pallas import tpu as pltpu
from jax.sharding import PartitionSpec as P

X = 128
D = 4
S = 4
D2 = D * D
TILE = D2 * D2
CHUNKS = X // D2
QUAD = 4
EPSILON = 1e-06

MESH = pl.DeviceIdType.MESH
BF16 = jnp.bfloat16
F32 = jnp.float32
NT = (((1,), (1,)), ((), ()))


def dot(a, b):
    return jnp.dot(a, b, preferred_element_type=F32)


def dot_nt(a, b):
    return lax.dot_general(a, b, NT, preferred_element_type=F32)


def iota(shape, dim):
    return lax.broadcasted_iota(jnp.int32, shape, dim)


def select(condition):
    return jnp.where(condition, 1.0, 0.0).astype(BF16)


def swap_16():
    rows, columns = iota((TILE, TILE), 0), iota((TILE, TILE), 1)
    return select(columns == ((rows & 15) << 4 | rows >> 4))


def double_layer(site, operator_ref, odd, ket_ref, bra_ref, total_ref):
    wide = jnp.concatenate([site, site], axis=1)
    rows, columns = iota(wide.shape, 0), iota(wide.shape, 1)
    shift = ((rows >> 2) - (columns >> 4)) & 3
    swapped = jnp.where(shift == 0, wide, 0.0)
    for k in range(1, D):
        moved = pltpu.roll(pltpu.roll(wide, D * k, 0), wide.shape[1] - D2 * k, 1)
        swapped = jnp.where(shift == k, moved, swapped)
    wide = jnp.where(odd == 1, swapped, wide)
    half = D * D2
    high = wide.astype(BF16)
    low = (wide - high.astype(F32)).astype(BF16)
    parts = jnp.where(columns < half, high.astype(F32), low.astype(F32)).astype(BF16)
    index, entry = iota((TILE, D2), 0), iota((TILE, D2), 1)
    ket_rows = select(entry == ((index >> 4 & 12) | (index >> 2 & 3)))
    bra_rows = select(entry == ((index >> 2 & 12) | (index & 3)))
    ket = dot(ket_rows, parts).astype(BF16)
    bra = dot(bra_rows, parts).astype(BF16)
    ket_ref[:, : 2 * half] = ket
    ket_ref[:, 2 * half :] = ket
    bra_ref[...] = bra
    total_ref[...] = jnp.zeros_like(total_ref)

    def add(t, carry):
        index, entry = iota((TILE, 4 * half), 0), iota((TILE, 4 * half), 1)
        ket_place = (index & 12) << 2 | (index >> 6) << 2
        bra_place = (index & 3) << 4 | (index >> 2 & 12)
        lanes = iota((8, 4 * half), 1)
        column = jnp.zeros(lanes.shape, F32)
        for s in range(S):
            column = jnp.where((lanes & 3) == s, operator_ref[0, s, t], column)
        high = column.astype(BF16).astype(F32)
        column = jnp.where(lanes < 2 * half, high, column - high)[:1]
        kets = jnp.where((entry & 60) == ket_place, column, 0.0).astype(BF16)
        bras = select((entry & 63) == bra_place + t)[:, : 2 * half]
        total_ref[...] += dot_nt(kets, ket_ref[...]) * dot_nt(bras, bra_ref[...])
        return carry

    lax.fori_loop(0, S, add, 0)
    return total_ref[...].astype(BF16)


def kernel(
    n_rows,
    n_columns,
    kept_ref,
    operator_hbm,
    site_hbm,
    front_hbm,
    factor_hbm,
    arrived_ref,
    divisor_ref,
    operator_ref,
    site_ref,
    front_ref,
    factor_ref,
    planes_ref,
    turned_ref,
    sent_ref,
    left_ref,
    relay_ref,
    front_planes_ref,
    swap_ref,
    identity_ref,
    ket_ref,
    bra_ref,
    total_ref,
    doubled_ref,
    projected_ref,
    absorbed_ref,
    unscaled_ref,
    quad_ref,
    ring_ref,
    load_sem,
    left_send,
    left_recv,
    relay_send,
    relay_recv,
    front_send,
    front_recv,
    quad_send,
    quad_recv,
    ring_send,
    ring_recv,
):
    n_ring = n_columns // QUAD
    row, column = lax.axis_index("rows"), lax.axis_index("cols")
    odd = lax.rem(row, 2)
    partner = row + 1 - 2 * odd
    before = lax.rem(column + n_columns - 1, n_columns)
    behind = lax.rem(column + 1, n_columns)
    place, member = column // QUAD, lax.rem(column, QUAD)
    core = lax.rem(column, 2)

    def beside_x(to_row, to_column, up):
        low = to_row // (n_rows // 2)
        flip = low if up else 1 - low
        start = (to_column // QUAD) * QUAD
        high = lax.rem(to_column, QUAD) // 2
        high = high + flip * (1 - 2 * high)
        return to_row + (n_rows // 2) * (1 - 2 * low), start + 2 * high + 1

    def load(source, target, k):
        copy = pltpu.make_async_copy(source, target, load_sem.at[k])
        copy.start()
        return copy

    load_factor = load(factor_hbm, factor_ref, 0)
    load_front = load(front_hbm, front_ref, 1)
    load_site = load(site_hbm, site_ref, 2)
    load_operator = load(operator_hbm, operator_ref, 3)

    barrier = pltpu.get_barrier_semaphore()

    def greet(to_row, to_column):
        pl.semaphore_signal(barrier, inc=1, device_id=(to_row, to_column), device_id_type=MESH)

    def quad_column(k):
        return place * QUAD + lax.rem(member + k, QUAD)

    def ring_column(k):
        return lax.rem(place + k, n_ring) * QUAD + member

    greet(row, before)
    greet(row, behind)
    greet(partner, column)
    for k in range(1, QUAD):
        greet(row, quad_column(k))

    def greet_ring(k, carry):
        greet(partner, ring_column(k))
        return carry

    lax.fori_loop(1, n_ring, greet_ring, 0)

    relay = beside_x(row, column, 0)
    served = beside_x(row, column, 1)
    served_target = served[0], lax.rem(served[1] + 1, n_columns)
    left_relay = beside_x(row, before, 0)

    @pl.when(core == 1)
    def _():
        greet(*served)

    @pl.when(core == 0)
    def _():
        greet(*left_relay)

    def chunk(ref, i):
        return ref.at[pl.ds(pl.multiple_of(i * TILE, TILE), TILE), :]

    def rows_of(i, size):
        return pl.ds(pl.multiple_of(i * size, size), size)

    def beside(ref, i):
        block = ref[rows_of(i, 2 * TILE), :]
        return jnp.concatenate([block[:TILE], block[TILE:]], axis=1)

    swap_ref[...] = swap_16()
    identity_ref[...] = select(iota((X, X), 0) == iota((X, X), 1))
    load_factor.wait()
    load_front.wait()

    def permute(i, carry):
        kept = (iota((TILE, 2 * X), 1) & (X - 1)) < kept_ref[0, 0]
        block = dot(swap_ref[...], beside(factor_ref, i))
        block = jnp.where(kept, block, 0.0).astype(BF16)
        other = dot(swap_ref[...], beside(front_ref, i)).astype(BF16)
        for k in range(2):
            lanes = slice(k * X, (k + 1) * X)
            for q in range(D2):
                start = pl.multiple_of(q * X + i * 2 * D2 + k * D2, D2)
                planes_ref[pl.ds(start, D2), :] = block[q * D2 : (q + 1) * D2, lanes]
            for v in range(D2):
                start = pl.multiple_of(i * 2 * D2 + k * D2, D2)
                front_planes_ref[pl.ds(start, D2), v * X : (v + 1) * X] = other[
                    v * D2 : (v + 1) * D2, lanes
                ]
        return carry

    lax.fori_loop(0, CHUNKS // 2, permute, 0)

    def turn(i, carry):
        for n in range(2):
            block = planes_ref[rows_of(2 * i + n, 2 * X), :]
            both = dot_nt(identity_ref[...], block).astype(BF16)
            for k in range(2):
                for j in range(CHUNKS):
                    start = pl.multiple_of(j * TILE + (4 * i + 2 * n + k) * D2, D2)
                    turned_ref[pl.ds(start, D2), :] = both[
                        j * D2 : (j + 1) * D2, k * X : (k + 1) * X
                    ]
        return carry

    lax.fori_loop(0, D2 // 4, turn, 0)

    def interleave(i, carry):
        for n in range(2):
            both = dot(swap_ref[...], beside(turned_ref, 2 * i + n)).astype(BF16)
            for k in range(2):
                sent_ref[rows_of(4 * i + 2 * n + k, TILE), :] = both[:, k * X : (k + 1) * X]
        return carry

    lax.fori_loop(0, CHUNKS // 4, interleave, 0)

    pl.semaphore_wait(barrier, 2 + 1 + (QUAD - 1) + (n_ring - 1) + 2 * core)

    def left_copy(i):
        return pltpu.make_async_remote_copy(
            src_ref=chunk(sent_ref, i),
            dst_ref=chunk(left_ref, i),
            send_sem=left_send.at[i],
            recv_sem=left_recv.at[i],
            device_id=(row, behind),
            device_id_type=MESH,
        )

    def relay_copy(i):
        return pltpu.make_async_remote_copy(
            src_ref=chunk(sent_ref, i),
            dst_ref=chunk(relay_ref, i // 2),
            send_sem=left_send.at[i],
            recv_sem=relay_recv.at[i // 2],
            device_id=relay,
            device_id_type=MESH,
        )

    def onward_copy(i):
        return pltpu.make_async_remote_copy(
            src_ref=chunk(relay_ref, i // 2),
            dst_ref=chunk(left_ref, i),
            send_sem=relay_send.at[i // 2],
            recv_sem=left_recv.at[i],
            device_id=served_target,
            device_id_type=MESH,
        )

    def send_left(i):
        left_copy(i).start()
        relay_copy(i + 1).start()

    def pass_on(i):
        relay_copy(i).wait_recv()
        onward_copy(i).start()

    def start_left(i, carry):
        left_copy(i).start()
        return carry

    @pl.when(core == 0)
    def _():
        lax.fori_loop(0, CHUNKS, start_left, 0)

    @pl.when(core == 1)
    def _():
        send_left(0)

    load_site.wait()
    load_operator.wait()
    doubled_ref[...] = double_layer(site_ref[0], operator_ref, odd, ket_ref, bra_ref, total_ref)

    @pl.when(core == 1)
    def _():
        send_left(2)
        pass_on(1)

    def front_copy(i):
        return pltpu.make_async_remote_copy(
            src_ref=chunk(unscaled_ref, i),
            dst_ref=chunk(arrived_ref, i),
            send_sem=front_send.at[i],
            recv_sem=front_recv.at[i],
            device_id=(partner, column),
            device_id_type=MESH,
        )

    def project(i):
        left = left_ref[rows_of(i, TILE), :]
        for v in range(0, D2, 2):
            both = dot(left, front_planes_ref[:, v * X : (v + 2) * X]).astype(BF16)
            for k in range(2):
                projected_ref[:, (v + k) * D2 : (v + k + 1) * D2, :] = both[
                    :, k * X : (k + 1) * X
                ].reshape(D2, D2, X)

    def absorb():
        for a in range(0, D2, 2):
            pair = jnp.concatenate([projected_ref[a], projected_ref[a + 1]], axis=1)
            both = dot(doubled_ref[...], pair).astype(BF16)
            for k in range(2):
                for q in range(D2):
                    absorbed_ref[(a + k) * D2 : (a + k + 1) * D2, q * X : (q + 1) * X] = both[
                        q * D2 : (q + 1) * D2, k * X : (k + 1) * X
                    ]

    def work(i, top):
        @pl.when(i < CHUNKS - 1)
        def _():
            left_copy(i + 1).wait_recv()

        @pl.when((core == 1) & (i < CHUNKS // 2 - 2))
        def _():
            send_left(2 * i + 4)

        @pl.when((core == 1) & (i >= 1) & (i < CHUNKS // 2))
        def _():
            pass_on(2 * i + 1)

        absorb()
        project(jnp.minimum(i + 1, CHUNKS - 1))
        result = dot(absorbed_ref[...], planes_ref[...])
        unscaled_ref[rows_of(i, TILE), :] = result.astype(BF16)
        front_copy(i).start()
        return jnp.maximum(top, jnp.max(jnp.abs(result).reshape(TILE // 8, 8, X), axis=0))

    left_copy(0).wait_recv()
    project(0)
    top = lax.fori_loop(0, CHUNKS, work, jnp.zeros((8, X), F32))
    top = jnp.max(top, axis=0, keepdims=True).astype(BF16).astype(F32)

    def quad_copy(k):
        return pltpu.make_async_remote_copy(
            src_ref=quad_ref.at[member],
            dst_ref=quad_ref.at[member],
            send_sem=quad_send.at[k],
            recv_sem=quad_recv.at[member],
            device_id=(row, quad_column(k)),
            device_id_type=MESH,
        )

    def arrival(ref, sems, slot):
        return pltpu.make_async_remote_copy(
            src_ref=ref.at[slot],
            dst_ref=ref.at[slot],
            send_sem=sems.at[slot],
            recv_sem=sems.at[slot],
            device_id=(row, behind),
            device_id_type=MESH,
        )

    quad_ref[member] = top
    for k in range(1, QUAD):
        quad_copy(k).start()
    for k in range(1, QUAD):
        arrival(quad_ref, quad_recv, lax.rem(member + k, QUAD)).wait_recv()
    for k in range(1, QUAD):
        quad_copy(k).wait_send()
    ring_ref[n_ring] = jnp.max(quad_ref[...], axis=0)

    def ring_copy(k):
        return pltpu.make_async_remote_copy(
            src_ref=ring_ref.at[n_ring],
            dst_ref=ring_ref.at[place],
            send_sem=ring_send.at[k],
            recv_sem=ring_recv.at[place],
            device_id=(partner, ring_column(k)),
            device_id_type=MESH,
        )

    def start_ring(k, carry):
        ring_copy(k).start()
        return carry

    def end_ring(k, carry):
        arrival(ring_ref, ring_recv, lax.rem(place + k, n_ring)).wait_recv()
        ring_copy(k).wait_send()
        return carry

    lax.fori_loop(0, n_ring, start_ring, 0)
    lax.fori_loop(0, n_ring, end_ring, 0)
    largest = jnp.max(ring_ref[:n_ring], axis=0)
    divisor_ref[...] = jnp.max(largest, axis=1, keepdims=True) + EPSILON

    def finish(i, carry):
        left_copy(i).wait_send()
        front_copy(i).wait()
        return carry

    lax.fori_loop(0, CHUNKS, finish, 0)

    @pl.when(core == 1)
    def _():
        for i in range(1, CHUNKS, 2):
            onward_copy(i).wait_send()


def per_device(fronts, factors, site_tensors, operators, kept_ranks):
    n_rows, n_columns = lax.axis_size("rows"), lax.axis_size("cols")
    rows = X * D2
    smem = pl.BlockSpec(memory_space=pltpu.SMEM)
    hbm = pl.BlockSpec(memory_space=pltpu.HBM)
    vmem = pl.BlockSpec(memory_space=pltpu.VMEM)
    anywhere = pl.BlockSpec(memory_space=pl.ANY)
    dma = pltpu.SemaphoreType.DMA

    def body(*refs):
        kernel(n_rows, n_columns, *refs)

    flops = 2 * 4 * X * X * X * D2 * D2
    arrived, divisor = pl.pallas_call(
        body,
        out_shape=(
            jax.ShapeDtypeStruct((rows, X), BF16),
            jax.ShapeDtypeStruct((1, 1), F32),
        ),
        in_specs=[smem] + [hbm] * 4,
        out_specs=(anywhere, vmem),
        scratch_shapes=[
            pltpu.SMEM(operators.shape, F32),
            pltpu.VMEM(site_tensors.shape, F32),
            pltpu.VMEM((rows, X), BF16),
            pltpu.VMEM((rows, X), BF16),
            pltpu.VMEM((rows, X), BF16),
            pltpu.VMEM((rows, X), BF16),
            pltpu.VMEM((rows, X), BF16),
            pltpu.VMEM((rows, X), BF16),
            pltpu.VMEM((rows // 2, X), BF16),
            pltpu.VMEM((X, rows), BF16),
            pltpu.VMEM((TILE, TILE), BF16),
            pltpu.VMEM((X, X), BF16),
            pltpu.VMEM((TILE, TILE), BF16),
            pltpu.VMEM((TILE, X), BF16),
            pltpu.VMEM((TILE, TILE), F32),
            pltpu.VMEM((TILE, TILE), BF16),
            pltpu.VMEM((D2, TILE, X), BF16),
            pltpu.VMEM((TILE, rows), BF16),
            pltpu.VMEM((rows, X), BF16),
            pltpu.VMEM((QUAD, 1, X), F32),
            pltpu.VMEM((n_columns // QUAD + 1, 1, X), F32),
            dma((4,)),
            dma((CHUNKS,)),
            dma((CHUNKS,)),
            dma((CHUNKS // 2,)),
            dma((CHUNKS // 2,)),
            dma((CHUNKS,)),
            dma((CHUNKS,)),
            dma((QUAD,)),
            dma((QUAD,)),
            dma((n_columns // QUAD,)),
            dma((n_columns // QUAD,)),
        ],
        compiler_params=pltpu.CompilerParams(
            collective_id=0, has_side_effects=True, vmem_limit_bytes=40 * 2**20
        ),
        cost_estimate=pl.CostEstimate(flops=flops, bytes_accessed=3 * 2**19, transcendentals=0),
    )(
        kept_ranks,
        *(
            pltpu.with_memory_space_constraint(operand, pltpu.HBM)
            for operand in (
                operators,
                site_tensors,
                fronts.reshape(rows, X),
                factors.reshape(rows, X),
            )
        )
    )
    normalized = arrived.astype(F32) / divisor[0, 0]
    return normalized.astype(BF16).reshape(1, X, D2, X)


def solution(mesh):
    return jax.shard_map(
        per_device,
        mesh=mesh,
        in_specs=(
            P("rows", None, None, "cols"),
            P("rows", None, "cols"),
            P("rows", None, "cols"),
            P("rows", None, "cols"),
            P("rows", "cols"),
        ),
        out_specs=P("rows", None, None, "cols"),
        check_vma=False,
    )
```

```python
import jax
import jax.numpy as jnp
from jax import lax
from jax.experimental import pallas as pl
from jax.experimental.pallas import tpu as pltpu
from jax.sharding import PartitionSpec as P

X = 128
D = 4
S = 4
D2 = D * D
TILE = D2 * D2
CHUNKS = X // D2
QUAD = 4
EPSILON = 1e-06

MESH = pl.DeviceIdType.MESH
BF16 = jnp.bfloat16
F32 = jnp.float32
NT = (((1,), (1,)), ((), ()))


def dot(a, b):
    return jnp.dot(a, b, preferred_element_type=F32)


def dot_nt(a, b):
    return lax.dot_general(a, b, NT, preferred_element_type=F32)


def iota(shape, dim):
    return lax.broadcasted_iota(jnp.int32, shape, dim)


def select(condition):
    return jnp.where(condition, 1.0, 0.0).astype(BF16)


def swap_16():
    rows, columns = iota((TILE, TILE), 0), iota((TILE, TILE), 1)
    return select(columns == ((rows & 15) << 4 | rows >> 4))


def double_layer(site, operator_ref, odd, ket_ref, bra_ref, total_ref):
    wide = jnp.concatenate([site, site], axis=1)
    rows, columns = iota(wide.shape, 0), iota(wide.shape, 1)
    shift = ((rows >> 2) - (columns >> 4)) & 3
    swapped = jnp.where(shift == 0, wide, 0.0)
    for k in range(1, D):
        moved = pltpu.roll(pltpu.roll(wide, D * k, 0), wide.shape[1] - D2 * k, 1)
        swapped = jnp.where(shift == k, moved, swapped)
    wide = jnp.where(odd == 1, swapped, wide)
    half = D * D2
    high = wide.astype(BF16)
    low = (wide - high.astype(F32)).astype(BF16)
    parts = jnp.where(columns < half, high.astype(F32), low.astype(F32)).astype(BF16)
    index, entry = iota((TILE, D2), 0), iota((TILE, D2), 1)
    ket_rows = select(entry == ((index >> 4 & 12) | (index >> 2 & 3)))
    bra_rows = select(entry == ((index >> 2 & 12) | (index & 3)))
    ket = dot(ket_rows, parts).astype(BF16)
    bra = dot(bra_rows, parts).astype(BF16)
    ket_ref[...] = ket
    bra_ref[...] = bra
    total_ref[...] = jnp.zeros_like(total_ref)

    def add(t, carry):
        index, entry = iota((TILE, 4 * half), 0), iota((TILE, 4 * half), 1)
        ket_place = (index & 12) << 2 | (index >> 6) << 2
        bra_place = (index & 3) << 4 | (index >> 2 & 12)
        lanes = iota((8, 4 * half), 1)
        column = jnp.zeros(lanes.shape, F32)
        for s in range(S):
            column = jnp.where((lanes & 3) == s, operator_ref[0, s, t], column)
        high = column.astype(BF16).astype(F32)
        column = jnp.where(lanes < 2 * half, high, column - high)[:1]
        kets = jnp.where((entry & 60) == ket_place, column, 0.0).astype(BF16)
        bras = select((entry & 63) == bra_place + t)[:, : 2 * half]
        total_ref[...] += dot_nt(kets, jnp.concatenate([ket_ref[...]] * 2, axis=1)) * dot_nt(bras, bra_ref[...])
        return carry

    lax.fori_loop(0, S, add, 0)
    return total_ref[...].astype(BF16)


def wide(ref):
    return jnp.concatenate([ref[i] for i in range(ref.shape[0])], axis=1)


def kernel(
    n_rows,
    n_columns,
    kept_ref,
    operator_hbm,
    site_hbm,
    front_hbm,
    factor_hbm,
    arrived_ref,
    divisor_ref,
    operator_ref,
    site_ref,
    front_ref,
    factor_ref,
    planes_ref,
    turned_ref,
    sent_ref,
    left_ref,
    relay_ref,
    front_planes_ref,
    swap_ref,
    identity_ref,
    ket_ref,
    bra_ref,
    total_ref,
    doubled_ref,
    projected_ref,
    absorbed_ref,
    unscaled_ref,
    quad_ref,
    ring_ref,
    load_sem,
    ready_sem,
    left_send,
    left_recv,
    relay_send,
    relay_recv,
    front_send,
    front_recv,
    quad_send,
    quad_recv,
    ring_send,
    ring_recv,
):
    n_ring = n_columns // QUAD
    row, column = lax.axis_index("rows"), lax.axis_index("cols")
    odd = lax.rem(row, 2)
    partner = row + 1 - 2 * odd
    before = lax.rem(column + n_columns - 1, n_columns)
    behind = lax.rem(column + 1, n_columns)
    place, member = column // QUAD, lax.rem(column, QUAD)
    core = lax.rem(column, 2)

    def beside_x(to_row, to_column, up):
        low = to_row // (n_rows // 2)
        flip = low if up else 1 - low
        start = (to_column // QUAD) * QUAD
        high = lax.rem(to_column, QUAD) // 2
        high = high + flip * (1 - 2 * high)
        return to_row + (n_rows // 2) * (1 - 2 * low), start + 2 * high + 1

    def load(source, target, k):
        copy = pltpu.make_async_copy(source, target, load_sem.at[k])
        copy.start()
        return copy

    def load_factor(i):
        piece = pl.ds(pl.multiple_of(i * 2 * TILE, 2 * TILE), 2 * TILE)
        return pltpu.make_async_copy(
            factor_hbm.at[piece, :], factor_ref.at[piece, :], load_sem.at[3 + i]
        )

    for i in range(CHUNKS // 2):
        load_factor(i).start()
    load_site = load(site_hbm, site_ref, 1)
    load_operator = load(operator_hbm, operator_ref, 2)
    load_front = load(front_hbm, front_ref, 0)

    barrier = pltpu.get_barrier_semaphore()

    def greet(to_row, to_column):
        pl.semaphore_signal(barrier, inc=1, device_id=(to_row, to_column), device_id_type=MESH)

    def quad_column(k):
        return place * QUAD + lax.rem(member + k, QUAD)

    def ring_column(k):
        return lax.rem(place + k + n_ring, n_ring) * QUAD + member

    greet(row, before)
    greet(row, behind)
    greet(partner, column)
    for k in range(1, QUAD):
        greet(row, quad_column(k))

    def far_first(k):
        return lax.rem(n_ring // 2 + n_ring + (2 * lax.rem(k, 2) - 1) * ((k + 1) // 2), n_ring)

    for k in (1, 2):
        greet(partner, ring_column(k))
        greet(partner, ring_column(-k))
    greet(row, ring_column(2))
    greet(row, ring_column(-2))

    def tell(n):
        for k in (-2 - 2 * n, 2 + 2 * n):
            pl.semaphore_signal(
                ready_sem.at[n],
                inc=1,
                device_id=(row, ring_column(k)),
                device_id_type=MESH,
            )

    relay = beside_x(row, column, 0)
    served = beside_x(row, column, 1)
    served_target = served[0], lax.rem(served[1] + 1, n_columns)
    left_relay = beside_x(row, before, 0)

    @pl.when(core == 1)
    def _():
        greet(*served)

    @pl.when(core == 0)
    def _():
        greet(*left_relay)

    def chunk(ref, i):
        return ref.at[pl.ds(pl.multiple_of(i * TILE, TILE), TILE), :]

    def rows_of(i, size):
        return pl.ds(pl.multiple_of(i * size, size), size)

    def beside(ref, i):
        block = ref[rows_of(i, 2 * TILE), :]
        return jnp.concatenate([block[:TILE], block[TILE:]], axis=1)

    swap = swap_16()
    swap_ref[0], swap_ref[1] = swap[:, :X], swap[:, X:]
    identity_ref[...] = select(iota((X, X), 0) == iota((X, X), 1))

    def permute(i, carry):
        load_factor(i).wait()
        kept = (iota((TILE, 2 * X), 1) & (X - 1)) < kept_ref[0, 0]
        block = dot(wide(swap_ref), beside(factor_ref, i))
        block = jnp.where(kept, block, 0.0).astype(BF16)
        for k in range(2):
            lanes = slice(k * X, (k + 1) * X)
            for q in range(D2):
                start = pl.multiple_of(q * X + i * 2 * D2 + k * D2, D2)
                planes_ref[pl.ds(start, D2), :] = block[q * D2 : (q + 1) * D2, lanes]
        return carry

    lax.fori_loop(0, CHUNKS // 2, permute, 0)

    def turn(i, carry):
        for n in range(2):
            block = planes_ref[rows_of(2 * i + n, 2 * X), :]
            both = dot_nt(identity_ref[...], block).astype(BF16)
            for k in range(2):
                for j in range(CHUNKS):
                    start = pl.multiple_of(j * TILE + (4 * i + 2 * n + k) * D2, D2)
                    turned_ref[pl.ds(start, D2), :] = both[
                        j * D2 : (j + 1) * D2, k * X : (k + 1) * X
                    ]
        return carry

    lax.fori_loop(0, D2 // 4, turn, 0)

    def interleave(i, carry):
        for n in range(2):
            both = dot(wide(swap_ref), beside(turned_ref, 2 * i + n)).astype(BF16)
            for k in range(2):
                sent_ref[rows_of(4 * i + 2 * n + k, TILE), :] = both[:, k * X : (k + 1) * X]
        return carry

    lax.fori_loop(0, CHUNKS // 4, interleave, 0)

    pl.semaphore_wait(barrier, 2 + 1 + (QUAD - 1) + 6 + 2 * core)
    tell(0)

    def left_copy(i):
        return pltpu.make_async_remote_copy(
            src_ref=chunk(sent_ref, i),
            dst_ref=chunk(left_ref, i),
            send_sem=left_send.at[i],
            recv_sem=left_recv.at[i],
            device_id=(row, behind),
            device_id_type=MESH,
        )

    def relay_copy(i):
        return pltpu.make_async_remote_copy(
            src_ref=chunk(sent_ref, i),
            dst_ref=chunk(relay_ref, i // 2),
            send_sem=left_send.at[i],
            recv_sem=relay_recv.at[i // 2],
            device_id=relay,
            device_id_type=MESH,
        )

    def onward_copy(i):
        return pltpu.make_async_remote_copy(
            src_ref=chunk(relay_ref, i // 2),
            dst_ref=chunk(left_ref, i),
            send_sem=relay_send.at[i // 2],
            recv_sem=left_recv.at[i],
            device_id=served_target,
            device_id_type=MESH,
        )

    def send_left(i):
        left_copy(i).start()
        relay_copy(i + 1).start()

    def pass_on(i):
        relay_copy(i).wait_recv()
        onward_copy(i).start()

    def start_left(i, carry):
        left_copy(i).start()
        return carry

    @pl.when(core == 0)
    def _():
        lax.fori_loop(0, CHUNKS, start_left, 0)

    @pl.when(core == 1)
    def _():
        send_left(0)

    def permute_front(i, carry):
        both = dot(wide(swap_ref), beside(front_ref, i)).astype(BF16)
        for k in range(2):
            for v in range(D2):
                start = pl.multiple_of(v * X + i * 2 * D2 + k * D2, D2)
                front_planes_ref[pl.ds(start, D2), :] = both[
                    v * D2 : (v + 1) * D2, k * X : (k + 1) * X
                ]
        return carry

    load_front.wait()
    lax.fori_loop(0, CHUNKS // 2, permute_front, 0)
    load_site.wait()
    load_operator.wait()
    doubled = double_layer(site_ref[0], operator_ref, odd, ket_ref, bra_ref, total_ref)
    doubled_ref[0], doubled_ref[1] = doubled[:, :X], doubled[:, X:]

    @pl.when(core == 1)
    def _():
        send_left(2)
        pass_on(1)

    def front_copy(i):
        return pltpu.make_async_remote_copy(
            src_ref=chunk(unscaled_ref, i),
            dst_ref=chunk(arrived_ref, i),
            send_sem=front_send.at[i],
            recv_sem=front_recv.at[i],
            device_id=(partner, column),
            device_id_type=MESH,
        )

    def project(i):
        left = left_ref[rows_of(i, TILE), :]
        for v in range(0, D2, 2):
            pair = jnp.concatenate(
                [front_planes_ref[v * X : (v + 1) * X], front_planes_ref[(v + 1) * X : (v + 2) * X]],
                axis=1,
            )
            both = dot(left, pair).astype(BF16)
            for k in range(2):
                projected_ref[:, (v + k) * D2 : (v + k + 1) * D2, :] = both[
                    :, k * X : (k + 1) * X
                ].reshape(D2, D2, X)

    def absorb():
        for a in range(0, D2, 2):
            pair = jnp.concatenate([projected_ref[a], projected_ref[a + 1]], axis=1)
            both = dot(wide(doubled_ref), pair).astype(BF16)
            for k in range(2):
                for q in range(D2):
                    absorbed_ref[q, (a + k) * D2 : (a + k + 1) * D2] = both[
                        q * D2 : (q + 1) * D2, k * X : (k + 1) * X
                    ]

    def work(i, top):
        @pl.when(i < CHUNKS - 1)
        def _():
            left_copy(i + 1).wait_recv()

        @pl.when((core == 1) & (i < CHUNKS // 2 - 2))
        def _():
            send_left(2 * i + 4)

        @pl.when((core == 1) & (i >= 1) & (i < CHUNKS // 2))
        def _():
            pass_on(2 * i + 1)

        @pl.when(i == 2)
        def _():
            pl.semaphore_wait(ready_sem.at[0], 2)
            tell(1)

        absorb()
        project(jnp.minimum(i + 1, CHUNKS - 1))
        result = dot(wide(absorbed_ref), planes_ref[...])
        unscaled_ref[rows_of(i, TILE), :] = result.astype(BF16)
        front_copy(i).start()
        return jnp.maximum(top, jnp.max(jnp.abs(result).reshape(TILE // 8, 8, X), axis=0))

    left_copy(0).wait_recv()
    project(0)
    top = lax.fori_loop(0, CHUNKS, work, jnp.zeros((8, X), F32))
    top = jnp.max(top, axis=0, keepdims=True).astype(BF16).astype(F32)

    def quad_copy(k):
        return pltpu.make_async_remote_copy(
            src_ref=quad_ref.at[member],
            dst_ref=quad_ref.at[member],
            send_sem=quad_send.at[k],
            recv_sem=quad_recv.at[member],
            device_id=(row, quad_column(k)),
            device_id_type=MESH,
        )

    def arrival(ref, sems, slot):
        return pltpu.make_async_remote_copy(
            src_ref=ref.at[slot],
            dst_ref=ref.at[slot],
            send_sem=sems.at[slot],
            recv_sem=sems.at[slot],
            device_id=(row, behind),
            device_id_type=MESH,
        )

    pl.semaphore_wait(ready_sem.at[1], 2)
    quad_ref[member] = top
    for k in range(1, QUAD):
        quad_copy(k).start()
    for k in range(1, QUAD):
        arrival(quad_ref, quad_recv, lax.rem(member + k, QUAD)).wait_recv()
    ring_ref[n_ring] = jnp.max(quad_ref[...], axis=0)

    def ring_copy(k):
        return pltpu.make_async_remote_copy(
            src_ref=ring_ref.at[n_ring],
            dst_ref=ring_ref.at[place],
            send_sem=ring_send.at[k],
            recv_sem=ring_recv.at[place],
            device_id=(partner, ring_column(k)),
            device_id_type=MESH,
        )

    def start_ring(k, carry):
        ring_copy(far_first(k)).start()
        return carry

    def end_ring(k, carry):
        arrival(ring_ref, ring_recv, lax.rem(place + k, n_ring)).wait_recv()
        ring_copy(k).wait_send()
        return carry

    lax.fori_loop(0, n_ring, start_ring, 0)
    lax.fori_loop(0, n_ring, end_ring, 0)
    largest = jnp.max(ring_ref[:n_ring], axis=0)
    divisor_ref[0, 0] = jnp.max(largest) + EPSILON

    for k in range(1, QUAD):
        quad_copy(k).wait_send()

    def finish(i, carry):
        left_copy(i).wait_send()
        front_copy(i).wait()
        return carry

    lax.fori_loop(0, CHUNKS, finish, 0)

    @pl.when(core == 1)
    def _():
        for i in range(1, CHUNKS, 2):
            onward_copy(i).wait_send()


def per_device(fronts, factors, site_tensors, operators, kept_ranks):
    n_rows, n_columns = lax.axis_size("rows"), lax.axis_size("cols")
    rows = X * D2
    smem = pl.BlockSpec(memory_space=pltpu.SMEM)
    hbm = pl.BlockSpec(memory_space=pltpu.HBM)
    anywhere = pl.BlockSpec(memory_space=pl.ANY)
    dma = pltpu.SemaphoreType.DMA

    def body(*refs):
        kernel(n_rows, n_columns, *refs)

    flops = 2 * 4 * X * X * X * D2 * D2
    arrived, divisor = pl.pallas_call(
        body,
        out_shape=(
            jax.ShapeDtypeStruct((rows, X), BF16),
            jax.ShapeDtypeStruct((1, 1), F32),
        ),
        in_specs=[smem] + [hbm] * 4,
        out_specs=(anywhere, smem),
        scratch_shapes=[
            pltpu.SMEM(operators.shape, F32),
            pltpu.VMEM(site_tensors.shape, F32),
            pltpu.VMEM((rows, X), BF16),
            pltpu.VMEM((rows, X), BF16),
            pltpu.VMEM((rows, X), BF16),
            pltpu.VMEM((rows, X), BF16),
            pltpu.VMEM((rows, X), BF16),
            pltpu.VMEM((rows, X), BF16),
            pltpu.VMEM((rows // 2, X), BF16),
            pltpu.VMEM((rows, X), BF16),
            pltpu.VMEM((2, TILE, X), BF16),
            pltpu.VMEM((X, X), BF16),
            pltpu.VMEM((TILE, X), BF16),
            pltpu.VMEM((TILE, X), BF16),
            pltpu.VMEM((TILE, TILE), F32),
            pltpu.VMEM((2, TILE, X), BF16),
            pltpu.VMEM((D2, TILE, X), BF16),
            pltpu.VMEM((D2, TILE, X), BF16),
            pltpu.VMEM((rows, X), BF16),
            pltpu.VMEM((QUAD, 1, X), F32),
            pltpu.VMEM((n_columns // QUAD + 1, 1, X), F32),
            dma((3 + CHUNKS // 2,)),
            pltpu.SemaphoreType.REGULAR((2,)),
            dma((CHUNKS,)),
            dma((CHUNKS,)),
            dma((CHUNKS // 2,)),
            dma((CHUNKS // 2,)),
            dma((CHUNKS,)),
            dma((CHUNKS,)),
            dma((QUAD,)),
            dma((QUAD,)),
            dma((n_columns // QUAD,)),
            dma((n_columns // QUAD,)),
        ],
        compiler_params=pltpu.CompilerParams(
            collective_id=0, has_side_effects=True, vmem_limit_bytes=40 * 2**20
        ),
        cost_estimate=pl.CostEstimate(flops=flops, bytes_accessed=3 * 2**19, transcendentals=0),
    )(
        kept_ranks,
        *(
            pltpu.with_memory_space_constraint(operand, pltpu.HBM)
            for operand in (
                operators,
                site_tensors,
                fronts.reshape(rows, X),
                factors.reshape(rows, X),
            )
        )
    )
    normalized = arrived.astype(F32) / divisor[0, 0]
    return normalized.astype(BF16).reshape(1, X, D2, X)


def solution(mesh):
    return jax.shard_map(
        per_device,
        mesh=mesh,
        in_specs=(
            P("rows", None, None, "cols"),
            P("rows", None, "cols"),
            P("rows", None, "cols"),
            P("rows", None, "cols"),
            P("rows", "cols"),
        ),
        out_specs=P("rows", None, None, "cols"),
        check_vma=False,
    )
```

```python
import jax
import jax.numpy as jnp
from jax import lax
from jax.experimental import pallas as pl
from jax.experimental.pallas import tpu as pltpu
from jax.sharding import PartitionSpec as P

X = 128
D = 4
S = 4
D2 = D * D
TILE = D2 * D2
CHUNKS = X // D2
QUAD = 4
EPSILON = 1e-06

MESH = pl.DeviceIdType.MESH
BF16 = jnp.bfloat16
F32 = jnp.float32
NT = (((1,), (1,)), ((), ()))


def dot(a, b):
    return jnp.dot(a, b, preferred_element_type=F32)


def dot_nt(a, b):
    return lax.dot_general(a, b, NT, preferred_element_type=F32)


def iota(shape, dim):
    return lax.broadcasted_iota(jnp.int32, shape, dim)


def select(condition):
    return jnp.where(condition, 1.0, 0.0).astype(BF16)


def swap_16():
    rows, columns = iota((TILE, TILE), 0), iota((TILE, TILE), 1)
    return select(columns == ((rows & 15) << 4 | rows >> 4))


def double_layer(site, operator_ref, odd, ket_ref, bra_ref, total_ref):
    wide = jnp.concatenate([site, site], axis=1)
    rows, columns = iota(wide.shape, 0), iota(wide.shape, 1)
    shift = ((rows >> 2) - (columns >> 4)) & 3
    swapped = jnp.where(shift == 0, wide, 0.0)
    for k in range(1, D):
        moved = pltpu.roll(pltpu.roll(wide, D * k, 0), wide.shape[1] - D2 * k, 1)
        swapped = jnp.where(shift == k, moved, swapped)
    wide = jnp.where(odd == 1, swapped, wide)
    half = D * D2
    high = wide.astype(BF16)
    low = (wide - high.astype(F32)).astype(BF16)
    parts = jnp.where(columns < half, high.astype(F32), low.astype(F32)).astype(BF16)
    index, entry = iota((TILE, D2), 0), iota((TILE, D2), 1)
    ket_rows = select(entry == ((index >> 4 & 12) | (index >> 2 & 3)))
    bra_rows = select(entry == ((index >> 2 & 12) | (index & 3)))
    ket = dot(ket_rows, parts).astype(BF16)
    bra = dot(bra_rows, parts).astype(BF16)
    ket_ref[...] = ket
    bra_ref[...] = bra
    total_ref[...] = jnp.zeros_like(total_ref)

    def add(t, carry):
        index, entry = iota((TILE, 4 * half), 0), iota((TILE, 4 * half), 1)
        ket_place = (index & 12) << 2 | (index >> 6) << 2
        bra_place = (index & 3) << 4 | (index >> 2 & 12)
        lanes = iota((8, 4 * half), 1)
        column = jnp.zeros(lanes.shape, F32)
        for s in range(S):
            column = jnp.where((lanes & 3) == s, operator_ref[0, s, t], column)
        high = column.astype(BF16).astype(F32)
        column = jnp.where(lanes < 2 * half, high, column - high)[:1]
        kets = jnp.where((entry & 60) == ket_place, column, 0.0).astype(BF16)
        bras = select((entry & 63) == bra_place + t)[:, : 2 * half]
        total_ref[...] += dot_nt(kets, jnp.concatenate([ket_ref[...]] * 2, axis=1)) * dot_nt(bras, bra_ref[...])
        return carry

    lax.fori_loop(0, S, add, 0)
    return total_ref[...].astype(BF16)


def wide(ref):
    return jnp.concatenate([ref[i] for i in range(ref.shape[0])], axis=1)


def kernel(
    n_rows,
    n_columns,
    kept_ref,
    operator_hbm,
    site_hbm,
    front_hbm,
    factor_hbm,
    arrived_ref,
    divisor_ref,
    operator_ref,
    site_ref,
    front_ref,
    factor_ref,
    planes_ref,
    turned_ref,
    sent_ref,
    left_ref,
    relay_ref,
    front_planes_ref,
    swap_ref,
    identity_ref,
    ket_ref,
    bra_ref,
    total_ref,
    doubled_ref,
    projected_ref,
    absorbed_ref,
    unscaled_ref,
    quad_ref,
    ring_ref,
    load_sem,
    ready_sem,
    left_send,
    left_recv,
    relay_send,
    relay_recv,
    front_send,
    front_recv,
    quad_send,
    quad_recv,
    ring_send,
    ring_recv,
):
    n_ring = n_columns // QUAD
    row, column = lax.axis_index("rows"), lax.axis_index("cols")
    odd = lax.rem(row, 2)
    partner = row + 1 - 2 * odd
    before = lax.rem(column + n_columns - 1, n_columns)
    behind = lax.rem(column + 1, n_columns)
    place, member = column // QUAD, lax.rem(column, QUAD)
    core = lax.rem(column, 2)

    def beside_x(to_row, to_column, up):
        low = to_row // (n_rows // 2)
        flip = low if up else 1 - low
        start = (to_column // QUAD) * QUAD
        high = lax.rem(to_column, QUAD) // 2
        high = high + flip * (1 - 2 * high)
        return to_row + (n_rows // 2) * (1 - 2 * low), start + 2 * high + 1

    def load(source, target, k):
        copy = pltpu.make_async_copy(source, target, load_sem.at[k])
        copy.start()
        return copy

    def load_factor(i):
        piece = pl.ds(pl.multiple_of(i * 2 * TILE, 2 * TILE), 2 * TILE)
        return pltpu.make_async_copy(
            factor_hbm.at[piece, :], factor_ref.at[piece, :], load_sem.at[3 + i]
        )

    for i in range(CHUNKS // 2):
        load_factor(i).start()
    load_site = load(site_hbm, site_ref, 1)
    load_operator = load(operator_hbm, operator_ref, 2)
    load_front = load(front_hbm, front_ref, 0)

    barrier = pltpu.get_barrier_semaphore()

    def greet(to_row, to_column):
        pl.semaphore_signal(barrier, inc=1, device_id=(to_row, to_column), device_id_type=MESH)

    def quad_column(k):
        return place * QUAD + lax.rem(member + k, QUAD)

    def ring_column(k):
        return lax.rem(place + k + n_ring, n_ring) * QUAD + member

    greet(row, before)
    greet(row, behind)
    greet(partner, column)
    for k in range(1, QUAD):
        greet(row, quad_column(k))

    def far_first(k):
        return lax.rem(n_ring // 2 + n_ring + (2 * lax.rem(k, 2) - 1) * ((k + 1) // 2), n_ring)

    for k in (1, 2):
        greet(partner, ring_column(k))
        greet(partner, ring_column(-k))
    greet(row, ring_column(2))
    greet(row, ring_column(-2))

    def tell(n):
        for k in (-2 - 2 * n, 2 + 2 * n):
            pl.semaphore_signal(
                ready_sem.at[n],
                inc=1,
                device_id=(row, ring_column(k)),
                device_id_type=MESH,
            )

    relay = beside_x(row, column, 0)
    served = beside_x(row, column, 1)
    served_target = served[0], lax.rem(served[1] + 1, n_columns)
    left_relay = beside_x(row, before, 0)

    @pl.when(core == 1)
    def _():
        greet(*served)

    @pl.when(core == 0)
    def _():
        greet(*left_relay)

    def chunk(ref, i):
        return ref.at[pl.ds(pl.multiple_of(i * TILE, TILE), TILE), :]

    def rows_of(i, size):
        return pl.ds(pl.multiple_of(i * size, size), size)

    def beside(ref, i):
        block = ref[rows_of(i, 2 * TILE), :]
        return jnp.concatenate([block[:TILE], block[TILE:]], axis=1)

    swap = swap_16()
    swap_ref[0], swap_ref[1] = swap[:, :X], swap[:, X:]
    identity_ref[...] = select(iota((X, X), 0) == iota((X, X), 1))

    def permute(i, carry):
        load_factor(i).wait()
        kept = (iota((TILE, 2 * X), 1) & (X - 1)) < kept_ref[0, 0]
        block = dot(wide(swap_ref), beside(factor_ref, i))
        block = jnp.where(kept, block, 0.0).astype(BF16)
        for k in range(2):
            lanes = slice(k * X, (k + 1) * X)
            for q in range(D2):
                start = pl.multiple_of(q * X + i * 2 * D2 + k * D2, D2)
                planes_ref[pl.ds(start, D2), :] = block[q * D2 : (q + 1) * D2, lanes]
        return carry

    lax.fori_loop(0, CHUNKS // 2, permute, 0)

    def turn(i, carry):
        for n in range(4):
            block = planes_ref[rows_of(4 * i + n, 2 * X), :]
            both = dot_nt(identity_ref[...], block).astype(BF16)
            for k in range(2):
                for j in range(CHUNKS):
                    start = pl.multiple_of(j * TILE + (8 * i + 2 * n + k) * D2, D2)
                    turned_ref[pl.ds(start, D2), :] = both[
                        j * D2 : (j + 1) * D2, k * X : (k + 1) * X
                    ]
        return carry

    lax.fori_loop(0, D2 // 8, turn, 0)

    for i in range(CHUNKS // 2):
        both = dot(wide(swap_ref), beside(turned_ref, i)).astype(BF16)
        for k in range(2):
            sent_ref[rows_of(2 * i + k, TILE), :] = both[:, k * X : (k + 1) * X]

    pl.semaphore_wait(barrier, 2 + 1 + (QUAD - 1) + 6 + 2 * core)
    tell(0)

    def left_copy(i):
        return pltpu.make_async_remote_copy(
            src_ref=chunk(sent_ref, i),
            dst_ref=chunk(left_ref, i),
            send_sem=left_send.at[i],
            recv_sem=left_recv.at[i],
            device_id=(row, behind),
            device_id_type=MESH,
        )

    def relay_copy(i):
        return pltpu.make_async_remote_copy(
            src_ref=chunk(sent_ref, i),
            dst_ref=chunk(relay_ref, i // 2 - 1),
            send_sem=left_send.at[i],
            recv_sem=relay_recv.at[i // 2 - 1],
            device_id=relay,
            device_id_type=MESH,
        )

    def onward_copy(i):
        return pltpu.make_async_remote_copy(
            src_ref=chunk(relay_ref, i // 2 - 1),
            dst_ref=chunk(left_ref, i),
            send_sem=relay_send.at[i // 2 - 1],
            recv_sem=left_recv.at[i],
            device_id=served_target,
            device_id_type=MESH,
        )

    def pass_on(i):
        relay_copy(i).wait_recv()
        onward_copy(i).start()

    def start_left(i, carry):
        left_copy(i).start()
        return carry

    @pl.when(core == 0)
    def _():
        lax.fori_loop(0, CHUNKS, start_left, 0)

    @pl.when(core == 1)
    def _():
        left_copy(0).start()
        relay_copy(2).start()

    def permute_front(i, carry):
        for n in range(2):
            both = dot(wide(swap_ref), beside(front_ref, 2 * i + n)).astype(BF16)
            for k in range(2):
                for v in range(D2):
                    start = pl.multiple_of(v * X + (4 * i + 2 * n + k) * D2, D2)
                    front_planes_ref[pl.ds(start, D2), :] = both[
                        v * D2 : (v + 1) * D2, k * X : (k + 1) * X
                    ]
        return carry

    load_front.wait()
    lax.fori_loop(0, CHUNKS // 4, permute_front, 0)

    @pl.when(core == 1)
    def _():
        left_copy(1).start()
        relay_copy(4).start()

    load_site.wait()
    load_operator.wait()
    doubled = double_layer(site_ref[0], operator_ref, odd, ket_ref, bra_ref, total_ref)
    doubled_ref[0], doubled_ref[1] = doubled[:, :X], doubled[:, X:]

    def front_copy(i):
        return pltpu.make_async_remote_copy(
            src_ref=chunk(unscaled_ref, i),
            dst_ref=chunk(arrived_ref, i),
            send_sem=front_send.at[i],
            recv_sem=front_recv.at[i],
            device_id=(partner, column),
            device_id_type=MESH,
        )

    def project(i):
        left = left_ref[rows_of(i, TILE), :]
        for v in range(0, D2, 2):
            pair = jnp.concatenate(
                [front_planes_ref[v * X : (v + 1) * X], front_planes_ref[(v + 1) * X : (v + 2) * X]],
                axis=1,
            )
            both = dot(left, pair).astype(BF16)
            for k in range(2):
                projected_ref[:, (v + k) * D2 : (v + k + 1) * D2, :] = both[
                    :, k * X : (k + 1) * X
                ].reshape(D2, D2, X)

    def absorb():
        for a in range(0, D2, 2):
            pair = jnp.concatenate([projected_ref[a], projected_ref[a + 1]], axis=1)
            both = dot(wide(doubled_ref), pair).astype(BF16)
            for k in range(2):
                for q in range(D2):
                    absorbed_ref[q, (a + k) * D2 : (a + k + 1) * D2] = both[
                        q * D2 : (q + 1) * D2, k * X : (k + 1) * X
                    ]

    def work(i, top):
        @pl.when(i < CHUNKS - 1)
        def _():
            left_copy(i + 1).wait_recv()

        @pl.when((core == 1) & (i < CHUNKS // 2 - 1))
        def _():
            pass_on(2 * i + 2)
            left_copy(2 * i + 3).start()

        @pl.when((core == 1) & (i == 0))
        def _():
            relay_copy(6).start()

        @pl.when(i == 2)
        def _():
            pl.semaphore_wait(ready_sem.at[0], 2)
            tell(1)

        absorb()
        project(jnp.minimum(i + 1, CHUNKS - 1))
        result = dot(wide(absorbed_ref), planes_ref[...])
        unscaled_ref[rows_of(i, TILE), :] = result.astype(BF16)
        front_copy(i).start()
        return jnp.maximum(top, jnp.max(jnp.abs(result).reshape(TILE // 8, 8, X), axis=0))

    left_copy(0).wait_recv()
    project(0)
    top = lax.fori_loop(0, CHUNKS, work, jnp.zeros((8, X), F32))
    top = jnp.max(top, axis=0, keepdims=True).astype(BF16).astype(F32)

    def quad_copy(k):
        return pltpu.make_async_remote_copy(
            src_ref=quad_ref.at[member],
            dst_ref=quad_ref.at[member],
            send_sem=quad_send.at[k],
            recv_sem=quad_recv.at[member],
            device_id=(row, quad_column(k)),
            device_id_type=MESH,
        )

    def arrival(ref, sems, slot):
        return pltpu.make_async_remote_copy(
            src_ref=ref.at[slot],
            dst_ref=ref.at[slot],
            send_sem=sems.at[slot],
            recv_sem=sems.at[slot],
            device_id=(row, behind),
            device_id_type=MESH,
        )

    pl.semaphore_wait(ready_sem.at[1], 2)
    quad_ref[member] = top
    for k in range(1, QUAD):
        quad_copy(k).start()
    for k in range(1, QUAD):
        arrival(quad_ref, quad_recv, lax.rem(member + k, QUAD)).wait_recv()
    ring_ref[n_ring] = jnp.max(quad_ref[...], axis=0)

    def ring_copy(k):
        return pltpu.make_async_remote_copy(
            src_ref=ring_ref.at[n_ring],
            dst_ref=ring_ref.at[place],
            send_sem=ring_send.at[k],
            recv_sem=ring_recv.at[place],
            device_id=(partner, ring_column(k)),
            device_id_type=MESH,
        )

    def start_ring(k, carry):
        ring_copy(far_first(k)).start()
        return carry

    def end_ring(k, carry):
        arrival(ring_ref, ring_recv, lax.rem(place + k, n_ring)).wait_recv()
        ring_copy(k).wait_send()
        return carry

    lax.fori_loop(0, n_ring, start_ring, 0)
    lax.fori_loop(0, n_ring, end_ring, 0)
    largest = jnp.max(ring_ref[:n_ring], axis=0)
    divisor_ref[0, 0] = jnp.max(largest) + EPSILON

    for k in range(1, QUAD):
        quad_copy(k).wait_send()

    def finish(i, carry):
        left_copy(i).wait_send()
        front_copy(i).wait()
        return carry

    lax.fori_loop(0, CHUNKS, finish, 0)

    @pl.when(core == 1)
    def _():
        for i in range(2, CHUNKS, 2):
            onward_copy(i).wait_send()


def per_device(fronts, factors, site_tensors, operators, kept_ranks):
    n_rows, n_columns = lax.axis_size("rows"), lax.axis_size("cols")
    rows = X * D2
    smem = pl.BlockSpec(memory_space=pltpu.SMEM)
    hbm = pl.BlockSpec(memory_space=pltpu.HBM)
    anywhere = pl.BlockSpec(memory_space=pl.ANY)
    dma = pltpu.SemaphoreType.DMA

    def body(*refs):
        kernel(n_rows, n_columns, *refs)

    flops = 2 * 4 * X * X * X * D2 * D2
    arrived, divisor = pl.pallas_call(
        body,
        out_shape=(
            jax.ShapeDtypeStruct((rows, X), BF16),
            jax.ShapeDtypeStruct((1, 1), F32),
        ),
        in_specs=[smem] + [hbm] * 4,
        out_specs=(anywhere, smem),
        scratch_shapes=[
            pltpu.SMEM(operators.shape, F32),
            pltpu.VMEM(site_tensors.shape, F32),
            pltpu.VMEM((rows, X), BF16),
            pltpu.VMEM((rows, X), BF16),
            pltpu.VMEM((rows, X), BF16),
            pltpu.VMEM((rows, X), BF16),
            pltpu.VMEM((rows, X), BF16),
            pltpu.VMEM((rows, X), BF16),
            pltpu.VMEM((rows // 2, X), BF16),
            pltpu.VMEM((rows, X), BF16),
            pltpu.VMEM((2, TILE, X), BF16),
            pltpu.VMEM((X, X), BF16),
            pltpu.VMEM((TILE, X), BF16),
            pltpu.VMEM((TILE, X), BF16),
            pltpu.VMEM((TILE, TILE), F32),
            pltpu.VMEM((2, TILE, X), BF16),
            pltpu.VMEM((D2, TILE, X), BF16),
            pltpu.VMEM((D2, TILE, X), BF16),
            pltpu.VMEM((rows, X), BF16),
            pltpu.VMEM((QUAD, 1, X), F32),
            pltpu.VMEM((n_columns // QUAD + 1, 1, X), F32),
            dma((3 + CHUNKS // 2,)),
            pltpu.SemaphoreType.REGULAR((2,)),
            dma((CHUNKS,)),
            dma((CHUNKS,)),
            dma((CHUNKS // 2,)),
            dma((CHUNKS // 2,)),
            dma((CHUNKS,)),
            dma((CHUNKS,)),
            dma((QUAD,)),
            dma((QUAD,)),
            dma((n_columns // QUAD,)),
            dma((n_columns // QUAD,)),
        ],
        compiler_params=pltpu.CompilerParams(
            collective_id=0, has_side_effects=True, vmem_limit_bytes=40 * 2**20
        ),
        cost_estimate=pl.CostEstimate(flops=flops, bytes_accessed=3 * 2**19, transcendentals=0),
    )(
        kept_ranks,
        *(
            pltpu.with_memory_space_constraint(operand, pltpu.HBM)
            for operand in (
                operators,
                site_tensors,
                fronts.reshape(rows, X),
                factors.reshape(rows, X),
            )
        )
    )
    normalized = arrived.astype(F32) / divisor[0, 0]
    return normalized.astype(BF16).reshape(1, X, D2, X)


def solution(mesh):
    return jax.shard_map(
        per_device,
        mesh=mesh,
        in_specs=(
            P("rows", None, None, "cols"),
            P("rows", None, "cols"),
            P("rows", None, "cols"),
            P("rows", None, "cols"),
            P("rows", "cols"),
        ),
        out_specs=P("rows", None, None, "cols"),
        check_vma=False,
    )
```

```python
import jax
import jax.numpy as jnp
from jax import lax
from jax.experimental import pallas as pl
from jax.experimental.pallas import tpu as pltpu
from jax.sharding import PartitionSpec as P

X = 128
D = 4
S = 4
D2 = D * D
TILE = D2 * D2
CHUNKS = X // D2
QUAD = 4
EPSILON = 1e-06

MESH = pl.DeviceIdType.MESH
BF16 = jnp.bfloat16
F32 = jnp.float32
NT = (((1,), (1,)), ((), ()))


def dot(a, b):
    return jnp.dot(a, b, preferred_element_type=F32)


def dot_nt(a, b):
    return lax.dot_general(a, b, NT, preferred_element_type=F32)


def iota(shape, dim):
    return lax.broadcasted_iota(jnp.int32, shape, dim)


def select(condition):
    return jnp.where(condition, 1.0, 0.0).astype(BF16)


def swap_16():
    rows, columns = iota((TILE, TILE), 0), iota((TILE, TILE), 1)
    return select(columns == ((rows & 15) << 4 | rows >> 4))


def double_layer(site, operator_ref, odd, ket_ref, bra_ref, total_ref):
    wide = jnp.concatenate([site, site], axis=1)
    rows, columns = iota(wide.shape, 0), iota(wide.shape, 1)
    shift = ((rows >> 2) - (columns >> 4)) & 3
    swapped = jnp.where(shift == 0, wide, 0.0)
    for k in range(1, D):
        moved = pltpu.roll(pltpu.roll(wide, D * k, 0), wide.shape[1] - D2 * k, 1)
        swapped = jnp.where(shift == k, moved, swapped)
    wide = jnp.where(odd == 1, swapped, wide)
    half = D * D2
    high = wide.astype(BF16)
    low = (wide - high.astype(F32)).astype(BF16)
    parts = jnp.where(columns < half, high.astype(F32), low.astype(F32)).astype(BF16)
    index, entry = iota((TILE, D2), 0), iota((TILE, D2), 1)
    ket_rows = select(entry == ((index >> 4 & 12) | (index >> 2 & 3)))
    bra_rows = select(entry == ((index >> 2 & 12) | (index & 3)))
    ket = dot(ket_rows, parts).astype(BF16)
    bra = dot(bra_rows, parts).astype(BF16)
    ket_ref[...] = ket
    bra_ref[...] = bra
    total_ref[...] = jnp.zeros_like(total_ref)

    def add(t, carry):
        index, entry = iota((TILE, 4 * half), 0), iota((TILE, 4 * half), 1)
        ket_place = (index & 12) << 2 | (index >> 6) << 2
        bra_place = (index & 3) << 4 | (index >> 2 & 12)
        lanes = iota((8, 4 * half), 1)
        column = jnp.zeros(lanes.shape, F32)
        for s in range(S):
            column = jnp.where((lanes & 3) == s, operator_ref[0, s, t], column)
        high = column.astype(BF16).astype(F32)
        column = jnp.where(lanes < 2 * half, high, column - high)[:1]
        kets = jnp.where((entry & 60) == ket_place, column, 0.0).astype(BF16)
        bras = select((entry & 63) == bra_place + t)[:, : 2 * half]
        total_ref[...] += dot_nt(kets, jnp.concatenate([ket_ref[...]] * 2, axis=1)) * dot_nt(bras, bra_ref[...])
        return carry

    lax.fori_loop(0, S, add, 0)
    return total_ref[...].astype(BF16)


def wide(ref):
    return jnp.concatenate([ref[i] for i in range(ref.shape[0])], axis=1)


def kernel(
    n_rows,
    n_columns,
    kept_ref,
    operator_hbm,
    site_hbm,
    front_hbm,
    factor_hbm,
    arrived_ref,
    divisor_ref,
    operator_ref,
    site_ref,
    front_ref,
    factor_ref,
    planes_ref,
    turned_ref,
    sent_ref,
    left_ref,
    relay_ref,
    front_planes_ref,
    swap_ref,
    identity_ref,
    ket_ref,
    bra_ref,
    total_ref,
    doubled_ref,
    projected_ref,
    absorbed_ref,
    unscaled_ref,
    quad_ref,
    ring_ref,
    load_sem,
    ready_sem,
    left_send,
    left_recv,
    relay_send,
    relay_recv,
    front_send,
    front_recv,
    quad_send,
    quad_recv,
    ring_send,
    ring_recv,
):
    n_ring = n_columns // QUAD
    row, column = lax.axis_index("rows"), lax.axis_index("cols")
    odd = lax.rem(row, 2)
    partner = row + 1 - 2 * odd
    before = lax.rem(column + n_columns - 1, n_columns)
    behind = lax.rem(column + 1, n_columns)
    place, member = column // QUAD, lax.rem(column, QUAD)
    core = lax.rem(column, 2)

    def beside_x(to_row, to_column, up):
        low = to_row // (n_rows // 2)
        flip = low if up else 1 - low
        start = (to_column // QUAD) * QUAD
        high = lax.rem(to_column, QUAD) // 2
        high = high + flip * (1 - 2 * high)
        return to_row + (n_rows // 2) * (1 - 2 * low), start + 2 * high + 1

    def load(source, target, k):
        copy = pltpu.make_async_copy(source, target, load_sem.at[k])
        copy.start()
        return copy

    def load_factor(i):
        piece = pl.ds(pl.multiple_of(i * 2 * TILE, 2 * TILE), 2 * TILE)
        return pltpu.make_async_copy(
            factor_hbm.at[piece, :], factor_ref.at[piece, :], load_sem.at[3 + i]
        )

    for i in range(CHUNKS // 2):
        load_factor(i).start()
    load_site = load(site_hbm, site_ref, 1)
    load_operator = load(operator_hbm, operator_ref, 2)
    load_front = load(front_hbm, front_ref, 0)

    barrier = pltpu.get_barrier_semaphore()

    def greet(to_row, to_column):
        pl.semaphore_signal(barrier, inc=1, device_id=(to_row, to_column), device_id_type=MESH)

    def quad_column(k):
        return place * QUAD + lax.rem(member + k, QUAD)

    def ring_column(k):
        return lax.rem(place + k + n_ring, n_ring) * QUAD + member

    greet(row, before)
    greet(row, behind)
    greet(partner, column)
    for k in range(1, QUAD):
        greet(row, quad_column(k))

    def far_first(k):
        return lax.rem(n_ring // 2 + n_ring + (2 * lax.rem(k, 2) - 1) * ((k + 1) // 2), n_ring)

    for k in (1, 2):
        greet(partner, ring_column(k))
        greet(partner, ring_column(-k))
    greet(row, ring_column(2))
    greet(row, ring_column(-2))

    def tell(n):
        for k in (-2 - 2 * n, 2 + 2 * n):
            pl.semaphore_signal(
                ready_sem.at[n],
                inc=1,
                device_id=(row, ring_column(k)),
                device_id_type=MESH,
            )

    relay = beside_x(row, column, 0)
    served = beside_x(row, column, 1)
    served_target = served[0], lax.rem(served[1] + 1, n_columns)
    left_relay = beside_x(row, before, 0)

    @pl.when(core == 1)
    def _():
        greet(*served)

    @pl.when(core == 0)
    def _():
        greet(*left_relay)

    def chunk(ref, i):
        return ref.at[pl.ds(pl.multiple_of(i * TILE, TILE), TILE), :]

    def rows_of(i, size):
        return pl.ds(pl.multiple_of(i * size, size), size)

    def beside(ref, i):
        block = ref[rows_of(i, 2 * TILE), :]
        return jnp.concatenate([block[:TILE], block[TILE:]], axis=1)

    swap = swap_16()
    swap_ref[0], swap_ref[1] = swap[:, :X], swap[:, X:]
    identity_ref[...] = select(iota((X, X), 0) == iota((X, X), 1))

    def permute(i, carry):
        load_factor(i).wait()
        kept = (iota((TILE, 2 * X), 1) & (X - 1)) < kept_ref[0, 0]
        block = dot(wide(swap_ref), beside(factor_ref, i))
        block = jnp.where(kept, block, 0.0).astype(BF16)
        for k in range(2):
            lanes = slice(k * X, (k + 1) * X)
            for q in range(D2):
                start = pl.multiple_of(q * X + i * 2 * D2 + k * D2, D2)
                planes_ref[pl.ds(start, D2), :] = block[q * D2 : (q + 1) * D2, lanes]
        return carry

    lax.fori_loop(0, CHUNKS // 2, permute, 0)

    def turn(i, carry):
        for n in range(4):
            block = planes_ref[rows_of(4 * i + n, 2 * X), :]
            both = dot_nt(identity_ref[...], block).astype(BF16)
            for k in range(2):
                for j in range(CHUNKS):
                    start = pl.multiple_of(j * TILE + (8 * i + 2 * n + k) * D2, D2)
                    turned_ref[pl.ds(start, D2), :] = both[
                        j * D2 : (j + 1) * D2, k * X : (k + 1) * X
                    ]
        return carry

    lax.fori_loop(0, D2 // 8, turn, 0)

    for i in range(CHUNKS // 2):
        both = dot(wide(swap_ref), beside(turned_ref, i)).astype(BF16)
        for k in range(2):
            sent_ref[rows_of(2 * i + k, TILE), :] = both[:, k * X : (k + 1) * X]

    pl.semaphore_wait(barrier, 2 + 1 + (QUAD - 1) + 6 + 2 * core)
    tell(0)

    def left_copy(i):
        return pltpu.make_async_remote_copy(
            src_ref=chunk(sent_ref, i),
            dst_ref=chunk(left_ref, i),
            send_sem=left_send.at[i],
            recv_sem=left_recv.at[i],
            device_id=(row, behind),
            device_id_type=MESH,
        )

    def relay_copy(i):
        return pltpu.make_async_remote_copy(
            src_ref=chunk(sent_ref, i),
            dst_ref=chunk(relay_ref, (i - 3) // 2),
            send_sem=left_send.at[i],
            recv_sem=relay_recv.at[(i - 3) // 2],
            device_id=relay,
            device_id_type=MESH,
        )

    def onward_copy(i):
        return pltpu.make_async_remote_copy(
            src_ref=chunk(relay_ref, (i - 3) // 2),
            dst_ref=chunk(left_ref, i),
            send_sem=relay_send.at[(i - 3) // 2],
            recv_sem=left_recv.at[i],
            device_id=served_target,
            device_id_type=MESH,
        )

    def pass_on(i):
        relay_copy(i).wait_recv()
        onward_copy(i).start()

    def start_left(i, carry):
        left_copy(i).start()
        return carry

    @pl.when(core == 0)
    def _():
        lax.fori_loop(0, CHUNKS, start_left, 0)

    @pl.when(core == 1)
    def _():
        left_copy(0).start()
        relay_copy(3).start()

    def permute_front(i, carry):
        for n in range(2):
            both = dot(wide(swap_ref), beside(front_ref, 2 * i + n)).astype(BF16)
            for k in range(2):
                for v in range(D2):
                    start = pl.multiple_of(v * X + (4 * i + 2 * n + k) * D2, D2)
                    front_planes_ref[pl.ds(start, D2), :] = both[
                        v * D2 : (v + 1) * D2, k * X : (k + 1) * X
                    ]
        return carry

    load_front.wait()
    lax.fori_loop(0, CHUNKS // 4, permute_front, 0)

    @pl.when(core == 1)
    def _():
        left_copy(1).start()
        relay_copy(5).start()

    load_site.wait()
    load_operator.wait()
    doubled = double_layer(site_ref[0], operator_ref, odd, ket_ref, bra_ref, total_ref)
    doubled_ref[0], doubled_ref[1] = doubled[:, :X], doubled[:, X:]

    @pl.when(core == 1)
    def _():
        left_copy(2).start()

    def front_copy(i):
        return pltpu.make_async_remote_copy(
            src_ref=chunk(unscaled_ref, i),
            dst_ref=chunk(arrived_ref, i),
            send_sem=front_send.at[i],
            recv_sem=front_recv.at[i],
            device_id=(partner, column),
            device_id_type=MESH,
        )

    def project(i):
        left = left_ref[rows_of(i, TILE), :]
        for v in range(0, D2, 4):
            four = [front_planes_ref[(v + k) * X : (v + k + 1) * X] for k in range(4)]
            result = dot(left, jnp.concatenate(four, axis=1)).astype(BF16)
            for k in range(4):
                projected_ref[:, (v + k) * D2 : (v + k + 1) * D2, :] = result[
                    :, k * X : (k + 1) * X
                ].reshape(D2, D2, X)

    def absorb():
        for a in range(0, D2, 4):
            four = [projected_ref[a + k] for k in range(4)]
            result = dot(wide(doubled_ref), jnp.concatenate(four, axis=1)).astype(BF16)
            for k in range(4):
                for q in range(D2):
                    absorbed_ref[q, (a + k) * D2 : (a + k + 1) * D2] = result[
                        q * D2 : (q + 1) * D2, k * X : (k + 1) * X
                    ]

    def work(i, top):
        @pl.when(i < CHUNKS - 1)
        def _():
            left_copy(i + 1).wait_recv()

        @pl.when((core == 1) & (i < 2))
        def _():
            pass_on(2 * i + 3)
            left_copy(2 * i + 4).start()

        @pl.when((core == 1) & (i == 0))
        def _():
            relay_copy(7).start()

        @pl.when((core == 1) & (i == 3))
        def _():
            pass_on(7)

        @pl.when(i == 2)
        def _():
            pl.semaphore_wait(ready_sem.at[0], 2)
            tell(1)

        absorb()
        project(jnp.minimum(i + 1, CHUNKS - 1))
        result = dot(wide(absorbed_ref), planes_ref[...])
        unscaled_ref[rows_of(i, TILE), :] = result.astype(BF16)
        front_copy(i).start()
        return jnp.maximum(top, jnp.max(jnp.abs(result).reshape(TILE // 8, 8, X), axis=0))

    left_copy(0).wait_recv()
    project(0)
    top = lax.fori_loop(0, CHUNKS, work, jnp.zeros((8, X), F32))
    top = jnp.max(top, axis=0, keepdims=True).astype(BF16).astype(F32)

    def quad_copy(k):
        return pltpu.make_async_remote_copy(
            src_ref=quad_ref.at[member],
            dst_ref=quad_ref.at[member],
            send_sem=quad_send.at[k],
            recv_sem=quad_recv.at[member],
            device_id=(row, quad_column(k)),
            device_id_type=MESH,
        )

    def arrival(ref, sems, slot):
        return pltpu.make_async_remote_copy(
            src_ref=ref.at[slot],
            dst_ref=ref.at[slot],
            send_sem=sems.at[slot],
            recv_sem=sems.at[slot],
            device_id=(row, behind),
            device_id_type=MESH,
        )

    pl.semaphore_wait(ready_sem.at[1], 2)
    quad_ref[member] = top
    for k in range(1, QUAD):
        quad_copy(k).start()
    for k in range(1, QUAD):
        arrival(quad_ref, quad_recv, lax.rem(member + k, QUAD)).wait_recv()
    ring_ref[n_ring] = jnp.max(quad_ref[...], axis=0)

    def ring_copy(k):
        return pltpu.make_async_remote_copy(
            src_ref=ring_ref.at[n_ring],
            dst_ref=ring_ref.at[place],
            send_sem=ring_send.at[k],
            recv_sem=ring_recv.at[place],
            device_id=(partner, ring_column(k)),
            device_id_type=MESH,
        )

    def start_ring(k, carry):
        ring_copy(far_first(k)).start()
        return carry

    def end_ring(k, carry):
        arrival(ring_ref, ring_recv, lax.rem(place + k, n_ring)).wait_recv()
        ring_copy(k).wait_send()
        return carry

    lax.fori_loop(0, n_ring, start_ring, 0)
    lax.fori_loop(0, n_ring, end_ring, 0)
    largest = jnp.max(ring_ref[:n_ring], axis=0)
    divisor_ref[0, 0] = jnp.max(largest) + EPSILON

    for k in range(1, QUAD):
        quad_copy(k).wait_send()

    def finish(i, carry):
        left_copy(i).wait_send()
        front_copy(i).wait()
        return carry

    lax.fori_loop(0, CHUNKS, finish, 0)

    @pl.when(core == 1)
    def _():
        for i in range(3, CHUNKS, 2):
            onward_copy(i).wait_send()


def per_device(fronts, factors, site_tensors, operators, kept_ranks):
    n_rows, n_columns = lax.axis_size("rows"), lax.axis_size("cols")
    rows = X * D2
    smem = pl.BlockSpec(memory_space=pltpu.SMEM)
    hbm = pl.BlockSpec(memory_space=pltpu.HBM)
    anywhere = pl.BlockSpec(memory_space=pl.ANY)
    dma = pltpu.SemaphoreType.DMA

    def body(*refs):
        kernel(n_rows, n_columns, *refs)

    flops = 2 * 4 * X * X * X * D2 * D2
    arrived, divisor = pl.pallas_call(
        body,
        out_shape=(
            jax.ShapeDtypeStruct((rows, X), BF16),
            jax.ShapeDtypeStruct((1, 1), F32),
        ),
        in_specs=[smem] + [hbm] * 4,
        out_specs=(anywhere, smem),
        scratch_shapes=[
            pltpu.SMEM(operators.shape, F32),
            pltpu.VMEM(site_tensors.shape, F32),
            pltpu.VMEM((rows, X), BF16),
            pltpu.VMEM((rows, X), BF16),
            pltpu.VMEM((rows, X), BF16),
            pltpu.VMEM((rows, X), BF16),
            pltpu.VMEM((rows, X), BF16),
            pltpu.VMEM((rows, X), BF16),
            pltpu.VMEM((rows // 2, X), BF16),
            pltpu.VMEM((rows, X), BF16),
            pltpu.VMEM((2, TILE, X), BF16),
            pltpu.VMEM((X, X), BF16),
            pltpu.VMEM((TILE, X), BF16),
            pltpu.VMEM((TILE, X), BF16),
            pltpu.VMEM((TILE, TILE), F32),
            pltpu.VMEM((2, TILE, X), BF16),
            pltpu.VMEM((D2, TILE, X), BF16),
            pltpu.VMEM((D2, TILE, X), BF16),
            pltpu.VMEM((rows, X), BF16),
            pltpu.VMEM((QUAD, 1, X), F32),
            pltpu.VMEM((n_columns // QUAD + 1, 1, X), F32),
            dma((3 + CHUNKS // 2,)),
            pltpu.SemaphoreType.REGULAR((2,)),
            dma((CHUNKS,)),
            dma((CHUNKS,)),
            dma((CHUNKS // 2,)),
            dma((CHUNKS // 2,)),
            dma((CHUNKS,)),
            dma((CHUNKS,)),
            dma((QUAD,)),
            dma((QUAD,)),
            dma((n_columns // QUAD,)),
            dma((n_columns // QUAD,)),
        ],
        compiler_params=pltpu.CompilerParams(
            collective_id=0, has_side_effects=True, vmem_limit_bytes=40 * 2**20
        ),
        cost_estimate=pl.CostEstimate(flops=flops, bytes_accessed=3 * 2**19, transcendentals=0),
    )(
        kept_ranks,
        *(
            pltpu.with_memory_space_constraint(operand, pltpu.HBM)
            for operand in (
                operators,
                site_tensors,
                fronts.reshape(rows, X),
                factors.reshape(rows, X),
            )
        )
    )
    normalized = arrived.astype(F32) / divisor[0, 0]
    return normalized.astype(BF16).reshape(1, X, D2, X)


def solution(mesh):
    return jax.shard_map(
        per_device,
        mesh=mesh,
        in_specs=(
            P("rows", None, None, "cols"),
            P("rows", None, "cols"),
            P("rows", None, "cols"),
            P("rows", None, "cols"),
            P("rows", "cols"),
        ),
        out_specs=P("rows", None, None, "cols"),
        check_vma=False,
    )
```

```python
import jax
import jax.numpy as jnp
from jax import lax
from jax.experimental import pallas as pl
from jax.experimental.pallas import tpu as pltpu
from jax.sharding import PartitionSpec as P

X = 128
D = 4
S = 4
D2 = D * D
TILE = D2 * D2
CHUNKS = X // D2
QUAD = 4
EPSILON = 1e-06

MESH = pl.DeviceIdType.MESH
BF16 = jnp.bfloat16
F32 = jnp.float32
NT = (((1,), (1,)), ((), ()))


def dot(a, b):
    return jnp.dot(a, b, preferred_element_type=F32)


def dot_nt(a, b):
    return lax.dot_general(a, b, NT, preferred_element_type=F32)


def iota(shape, dim):
    return lax.broadcasted_iota(jnp.int32, shape, dim)


def select(condition):
    return jnp.where(condition, 1.0, 0.0).astype(BF16)


def swap_16():
    rows, columns = iota((TILE, TILE), 0), iota((TILE, TILE), 1)
    return select(columns == ((rows & 15) << 4 | rows >> 4))


def double_layer(site, operator_ref, odd, ket_ref, bra_ref, total_ref):
    wide = jnp.concatenate([site, site], axis=1)
    rows, columns = iota(wide.shape, 0), iota(wide.shape, 1)
    shift = ((rows >> 2) - (columns >> 4)) & 3
    swapped = jnp.where(shift == 0, wide, 0.0)
    for k in range(1, D):
        moved = pltpu.roll(pltpu.roll(wide, D * k, 0), wide.shape[1] - D2 * k, 1)
        swapped = jnp.where(shift == k, moved, swapped)
    wide = jnp.where(odd == 1, swapped, wide)
    half = D * D2
    high = wide.astype(BF16)
    low = (wide - high.astype(F32)).astype(BF16)
    parts = jnp.where(columns < half, high.astype(F32), low.astype(F32)).astype(BF16)
    index, entry = iota((TILE, D2), 0), iota((TILE, D2), 1)
    ket_rows = select(entry == ((index >> 4 & 12) | (index >> 2 & 3)))
    bra_rows = select(entry == ((index >> 2 & 12) | (index & 3)))
    ket = dot(ket_rows, parts).astype(BF16)
    bra = dot(bra_rows, parts).astype(BF16)
    ket_ref[...] = ket
    bra_ref[...] = bra
    total_ref[...] = jnp.zeros_like(total_ref)

    def add(t, carry):
        index, entry = iota((TILE, 4 * half), 0), iota((TILE, 4 * half), 1)
        ket_place = (index & 12) << 2 | (index >> 6) << 2
        bra_place = (index & 3) << 4 | (index >> 2 & 12)
        lanes = iota((8, 4 * half), 1)
        column = jnp.zeros(lanes.shape, F32)
        for s in range(S):
            column = jnp.where((lanes & 3) == s, operator_ref[0, s, t], column)
        high = column.astype(BF16).astype(F32)
        column = jnp.where(lanes < 2 * half, high, column - high)[:1]
        kets = jnp.where((entry & 60) == ket_place, column, 0.0).astype(BF16)
        bras = select((entry & 63) == bra_place + t)[:, : 2 * half]
        total_ref[...] += dot_nt(kets, jnp.concatenate([ket_ref[...]] * 2, axis=1)) * dot_nt(bras, bra_ref[...])
        return carry

    lax.fori_loop(0, S, add, 0)
    return total_ref[...].astype(BF16)


def wide(ref):
    return jnp.concatenate([ref[i] for i in range(ref.shape[0])], axis=1)


def kernel(
    n_rows,
    n_columns,
    kept_ref,
    operator_hbm,
    site_hbm,
    front_hbm,
    factor_hbm,
    arrived_ref,
    divisor_ref,
    operator_ref,
    site_ref,
    front_ref,
    factor_ref,
    planes_ref,
    turned_ref,
    sent_ref,
    left_ref,
    relay_ref,
    front_planes_ref,
    swap_ref,
    identity_ref,
    ket_ref,
    bra_ref,
    total_ref,
    doubled_ref,
    projected_ref,
    absorbed_ref,
    unscaled_ref,
    quad_ref,
    ring_ref,
    load_sem,
    ready_sem,
    left_send,
    left_recv,
    relay_send,
    relay_recv,
    front_send,
    front_recv,
    quad_send,
    quad_recv,
    ring_send,
    ring_recv,
):
    n_ring = n_columns // QUAD
    row, column = lax.axis_index("rows"), lax.axis_index("cols")
    odd = lax.rem(row, 2)
    partner = row + 1 - 2 * odd
    before = lax.rem(column + n_columns - 1, n_columns)
    behind = lax.rem(column + 1, n_columns)
    place, member = column // QUAD, lax.rem(column, QUAD)
    core = lax.rem(column, 2)

    def beside_x(to_row, to_column, up):
        low = to_row // (n_rows // 2)
        flip = low if up else 1 - low
        start = (to_column // QUAD) * QUAD
        high = lax.rem(to_column, QUAD) // 2
        high = high + flip * (1 - 2 * high)
        return to_row + (n_rows // 2) * (1 - 2 * low), start + 2 * high + 1

    def load(source, target, k):
        copy = pltpu.make_async_copy(source, target, load_sem.at[k])
        copy.start()
        return copy

    def load_factor(i):
        piece = pl.ds(pl.multiple_of(i * 2 * TILE, 2 * TILE), 2 * TILE)
        return pltpu.make_async_copy(
            factor_hbm.at[piece, :], factor_ref.at[piece, :], load_sem.at[3 + i]
        )

    for i in range(CHUNKS // 2):
        load_factor(i).start()
    load_site = load(site_hbm, site_ref, 1)
    load_operator = load(operator_hbm, operator_ref, 2)
    load_front = load(front_hbm, front_ref, 0)

    barrier = pltpu.get_barrier_semaphore()

    def greet(to_row, to_column):
        pl.semaphore_signal(barrier, inc=1, device_id=(to_row, to_column), device_id_type=MESH)

    def quad_column(k):
        return place * QUAD + lax.rem(member + k, QUAD)

    def ring_column(k):
        return lax.rem(place + k + n_ring, n_ring) * QUAD + member

    greet(row, before)
    greet(row, behind)
    greet(partner, column)
    for k in range(1, QUAD):
        greet(row, quad_column(k))

    def far_first(k):
        return lax.rem(n_ring // 2 + n_ring + (2 * lax.rem(k, 2) - 1) * ((k + 1) // 2), n_ring)

    for k in (1, 2):
        greet(partner, ring_column(k))
        greet(partner, ring_column(-k))
    greet(row, ring_column(2))
    greet(row, ring_column(-2))

    def tell(n):
        for k in (-2 - 2 * n, 2 + 2 * n):
            pl.semaphore_signal(
                ready_sem.at[n],
                inc=1,
                device_id=(row, ring_column(k)),
                device_id_type=MESH,
            )

    relay = beside_x(row, column, 0)
    served = beside_x(row, column, 1)
    served_target = served[0], lax.rem(served[1] + 1, n_columns)
    left_relay = beside_x(row, before, 0)

    @pl.when(core == 1)
    def _():
        greet(*served)

    @pl.when(core == 0)
    def _():
        greet(*left_relay)

    def chunk(ref, i):
        return ref.at[pl.ds(pl.multiple_of(i * TILE, TILE), TILE), :]

    def rows_of(i, size):
        return pl.ds(pl.multiple_of(i * size, size), size)

    def beside(ref, i):
        block = ref[rows_of(i, 2 * TILE), :]
        return jnp.concatenate([block[:TILE], block[TILE:]], axis=1)

    swap = swap_16()
    swap_ref[0], swap_ref[1] = swap[:, :X], swap[:, X:]
    identity_ref[...] = select(iota((X, X), 0) == iota((X, X), 1))

    def permute(i, carry):
        load_factor(i).wait()
        kept = (iota((TILE, 2 * X), 1) & (X - 1)) < kept_ref[0, 0]
        block = dot(wide(swap_ref), beside(factor_ref, i))
        block = jnp.where(kept, block, 0.0).astype(BF16)
        for k in range(2):
            lanes = slice(k * X, (k + 1) * X)
            for q in range(D2):
                start = pl.multiple_of(q * X + i * 2 * D2 + k * D2, D2)
                planes_ref[pl.ds(start, D2), :] = block[q * D2 : (q + 1) * D2, lanes]
        return carry

    lax.fori_loop(0, CHUNKS // 2, permute, 0)

    def turn(i, carry):
        for n in range(4):
            block = planes_ref[rows_of(4 * i + n, 2 * X), :]
            both = dot_nt(identity_ref[...], block).astype(BF16)
            for k in range(2):
                for j in range(CHUNKS):
                    start = pl.multiple_of(j * TILE + (8 * i + 2 * n + k) * D2, D2)
                    turned_ref[pl.ds(start, D2), :] = both[
                        j * D2 : (j + 1) * D2, k * X : (k + 1) * X
                    ]
        return carry

    lax.fori_loop(0, D2 // 8, turn, 0)

    def interleave(i):
        both = dot(wide(swap_ref), beside(turned_ref, i)).astype(BF16)
        for k in range(2):
            sent_ref[rows_of(2 * i + k, TILE), :] = both[:, k * X : (k + 1) * X]

    interleave(0)
    pl.semaphore_wait(barrier, 2 + 1 + (QUAD - 1) + 6 + 2 * core)
    tell(0)

    def left_copy(i):
        return pltpu.make_async_remote_copy(
            src_ref=chunk(sent_ref, i),
            dst_ref=chunk(left_ref, i),
            send_sem=left_send.at[i],
            recv_sem=left_recv.at[i],
            device_id=(row, behind),
            device_id_type=MESH,
        )

    def relay_copy(i):
        return pltpu.make_async_remote_copy(
            src_ref=chunk(sent_ref, i),
            dst_ref=chunk(relay_ref, (i - 3) // 2),
            send_sem=left_send.at[i],
            recv_sem=relay_recv.at[(i - 3) // 2],
            device_id=relay,
            device_id_type=MESH,
        )

    def onward_copy(i):
        return pltpu.make_async_remote_copy(
            src_ref=chunk(relay_ref, (i - 3) // 2),
            dst_ref=chunk(left_ref, i),
            send_sem=relay_send.at[(i - 3) // 2],
            recv_sem=left_recv.at[i],
            device_id=served_target,
            device_id_type=MESH,
        )

    def pass_on(i):
        relay_copy(i).wait_recv()
        onward_copy(i).start()

    def start_left(i, carry):
        left_copy(i).start()
        return carry

    left_copy(0).start()
    for i in range(1, CHUNKS // 2):
        interleave(i)

    @pl.when(core == 0)
    def _():
        lax.fori_loop(1, CHUNKS, start_left, 0)

    @pl.when(core == 1)
    def _():
        relay_copy(3).start()

    def permute_front(i, carry):
        for n in range(2):
            both = dot(wide(swap_ref), beside(front_ref, 2 * i + n)).astype(BF16)
            for k in range(2):
                for v in range(D2):
                    start = pl.multiple_of(v * X + (4 * i + 2 * n + k) * D2, D2)
                    front_planes_ref[pl.ds(start, D2), :] = both[
                        v * D2 : (v + 1) * D2, k * X : (k + 1) * X
                    ]
        return carry

    load_front.wait()
    lax.fori_loop(0, CHUNKS // 4, permute_front, 0)

    @pl.when(core == 1)
    def _():
        left_copy(1).start()
        relay_copy(5).start()

    load_site.wait()
    load_operator.wait()
    doubled = double_layer(site_ref[0], operator_ref, odd, ket_ref, bra_ref, total_ref)
    doubled_ref[0], doubled_ref[1] = doubled[:, :X], doubled[:, X:]

    @pl.when(core == 1)
    def _():
        left_copy(2).start()

    def front_copy(i):
        return pltpu.make_async_remote_copy(
            src_ref=chunk(unscaled_ref, i),
            dst_ref=chunk(arrived_ref, i),
            send_sem=front_send.at[i],
            recv_sem=front_recv.at[i],
            device_id=(partner, column),
            device_id_type=MESH,
        )

    def project(i):
        left = left_ref[rows_of(i, TILE), :]
        for v in range(0, D2, 4):
            four = [front_planes_ref[(v + k) * X : (v + k + 1) * X] for k in range(4)]
            result = dot(left, jnp.concatenate(four, axis=1)).astype(BF16)
            for k in range(4):
                projected_ref[:, (v + k) * D2 : (v + k + 1) * D2, :] = result[
                    :, k * X : (k + 1) * X
                ].reshape(D2, D2, X)

    def absorb():
        for a in range(0, D2, 4):
            four = [projected_ref[a + k] for k in range(4)]
            result = dot(wide(doubled_ref), jnp.concatenate(four, axis=1)).astype(BF16)
            for k in range(4):
                for q in range(D2):
                    absorbed_ref[q, (a + k) * D2 : (a + k + 1) * D2] = result[
                        q * D2 : (q + 1) * D2, k * X : (k + 1) * X
                    ]

    def work(i, top):
        @pl.when(i < CHUNKS - 1)
        def _():
            left_copy(i + 1).wait_recv()

        @pl.when((core == 1) & (i < 2))
        def _():
            pass_on(2 * i + 3)
            left_copy(2 * i + 4).start()

        @pl.when((core == 1) & (i == 0))
        def _():
            relay_copy(7).start()

        @pl.when((core == 1) & (i == 3))
        def _():
            pass_on(7)

        @pl.when(i == 2)
        def _():
            pl.semaphore_wait(ready_sem.at[0], 2)
            tell(1)

        absorb()
        project(jnp.minimum(i + 1, CHUNKS - 1))
        result = dot(wide(absorbed_ref), planes_ref[...])
        unscaled_ref[rows_of(i, TILE), :] = result.astype(BF16)
        front_copy(i).start()
        return jnp.maximum(top, jnp.max(jnp.abs(result).reshape(TILE // 8, 8, X), axis=0))

    left_copy(0).wait_recv()
    project(0)
    top = lax.fori_loop(0, CHUNKS, work, jnp.zeros((8, X), F32))
    top = jnp.max(top, axis=0, keepdims=True).astype(BF16).astype(F32)

    def quad_copy(k):
        return pltpu.make_async_remote_copy(
            src_ref=quad_ref.at[member],
            dst_ref=quad_ref.at[member],
            send_sem=quad_send.at[k],
            recv_sem=quad_recv.at[member],
            device_id=(row, quad_column(k)),
            device_id_type=MESH,
        )

    def arrival(ref, sems, slot):
        return pltpu.make_async_remote_copy(
            src_ref=ref.at[slot],
            dst_ref=ref.at[slot],
            send_sem=sems.at[slot],
            recv_sem=sems.at[slot],
            device_id=(row, behind),
            device_id_type=MESH,
        )

    pl.semaphore_wait(ready_sem.at[1], 2)
    quad_ref[member] = top
    for k in range(1, QUAD):
        quad_copy(k).start()
    for k in range(1, QUAD):
        arrival(quad_ref, quad_recv, lax.rem(member + k, QUAD)).wait_recv()
    ring_ref[n_ring] = jnp.max(quad_ref[...], axis=0)

    def ring_copy(k):
        return pltpu.make_async_remote_copy(
            src_ref=ring_ref.at[n_ring],
            dst_ref=ring_ref.at[place],
            send_sem=ring_send.at[k],
            recv_sem=ring_recv.at[place],
            device_id=(partner, ring_column(k)),
            device_id_type=MESH,
        )

    def start_ring(k, carry):
        ring_copy(far_first(k)).start()
        return carry

    def end_ring(k, carry):
        arrival(ring_ref, ring_recv, lax.rem(place + k, n_ring)).wait_recv()
        ring_copy(k).wait_send()
        return carry

    lax.fori_loop(0, n_ring, start_ring, 0)
    lax.fori_loop(0, n_ring, end_ring, 0)
    largest = jnp.max(ring_ref[:n_ring], axis=0)
    divisor_ref[0, 0] = jnp.max(largest) + EPSILON

    for k in range(1, QUAD):
        quad_copy(k).wait_send()

    def finish(i, carry):
        left_copy(i).wait_send()
        front_copy(i).wait()
        return carry

    lax.fori_loop(0, CHUNKS, finish, 0)

    @pl.when(core == 1)
    def _():
        for i in range(3, CHUNKS, 2):
            onward_copy(i).wait_send()


def per_device(fronts, factors, site_tensors, operators, kept_ranks):
    n_rows, n_columns = lax.axis_size("rows"), lax.axis_size("cols")
    rows = X * D2
    smem = pl.BlockSpec(memory_space=pltpu.SMEM)
    hbm = pl.BlockSpec(memory_space=pltpu.HBM)
    anywhere = pl.BlockSpec(memory_space=pl.ANY)
    dma = pltpu.SemaphoreType.DMA

    def body(*refs):
        kernel(n_rows, n_columns, *refs)

    flops = 2 * 4 * X * X * X * D2 * D2
    arrived, divisor = pl.pallas_call(
        body,
        out_shape=(
            jax.ShapeDtypeStruct((rows, X), BF16),
            jax.ShapeDtypeStruct((1, 1), F32),
        ),
        in_specs=[smem] + [hbm] * 4,
        out_specs=(anywhere, smem),
        scratch_shapes=[
            pltpu.SMEM(operators.shape, F32),
            pltpu.VMEM(site_tensors.shape, F32),
            pltpu.VMEM((rows, X), BF16),
            pltpu.VMEM((rows, X), BF16),
            pltpu.VMEM((rows, X), BF16),
            pltpu.VMEM((rows, X), BF16),
            pltpu.VMEM((rows, X), BF16),
            pltpu.VMEM((rows, X), BF16),
            pltpu.VMEM((rows // 2, X), BF16),
            pltpu.VMEM((rows, X), BF16),
            pltpu.VMEM((2, TILE, X), BF16),
            pltpu.VMEM((X, X), BF16),
            pltpu.VMEM((TILE, X), BF16),
            pltpu.VMEM((TILE, X), BF16),
            pltpu.VMEM((TILE, TILE), F32),
            pltpu.VMEM((2, TILE, X), BF16),
            pltpu.VMEM((D2, TILE, X), BF16),
            pltpu.VMEM((D2, TILE, X), BF16),
            pltpu.VMEM((rows, X), BF16),
            pltpu.VMEM((QUAD, 1, X), F32),
            pltpu.VMEM((n_columns // QUAD + 1, 1, X), F32),
            dma((3 + CHUNKS // 2,)),
            pltpu.SemaphoreType.REGULAR((2,)),
            dma((CHUNKS,)),
            dma((CHUNKS,)),
            dma((CHUNKS // 2,)),
            dma((CHUNKS // 2,)),
            dma((CHUNKS,)),
            dma((CHUNKS,)),
            dma((QUAD,)),
            dma((QUAD,)),
            dma((n_columns // QUAD,)),
            dma((n_columns // QUAD,)),
        ],
        compiler_params=pltpu.CompilerParams(
            collective_id=0, has_side_effects=True, vmem_limit_bytes=40 * 2**20
        ),
        cost_estimate=pl.CostEstimate(flops=flops, bytes_accessed=3 * 2**19, transcendentals=0),
    )(
        kept_ranks,
        *(
            pltpu.with_memory_space_constraint(operand, pltpu.HBM)
            for operand in (
                operators,
                site_tensors,
                fronts.reshape(rows, X),
                factors.reshape(rows, X),
            )
        )
    )
    normalized = arrived.astype(F32) / divisor[0, 0]
    return normalized.astype(BF16).reshape(1, X, D2, X)


def solution(mesh):
    return jax.shard_map(
        per_device,
        mesh=mesh,
        in_specs=(
            P("rows", None, None, "cols"),
            P("rows", None, "cols"),
            P("rows", None, "cols"),
            P("rows", None, "cols"),
            P("rows", "cols"),
        ),
        out_specs=P("rows", None, None, "cols"),
        check_vma=False,
    )
```

```python
import jax
import jax.numpy as jnp
from jax import lax
from jax.experimental import pallas as pl
from jax.experimental.pallas import tpu as pltpu
from jax.sharding import PartitionSpec as P

X = 128
D = 4
S = 4
D2 = D * D
TILE = D2 * D2
CHUNKS = X // D2
QUAD = 4
EPSILON = 1e-06

MESH = pl.DeviceIdType.MESH
BF16 = jnp.bfloat16
F32 = jnp.float32
NT = (((1,), (1,)), ((), ()))


def dot(a, b):
    return jnp.dot(a, b, preferred_element_type=F32)


def dot_nt(a, b):
    return lax.dot_general(a, b, NT, preferred_element_type=F32)


def iota(shape, dim):
    return lax.broadcasted_iota(jnp.int32, shape, dim)


def select(condition):
    return jnp.where(condition, 1.0, 0.0).astype(BF16)


def swap_16():
    rows, columns = iota((TILE, TILE), 0), iota((TILE, TILE), 1)
    return select(columns == ((rows & 15) << 4 | rows >> 4))


def double_layer(site, operator_ref, odd, ket_ref, bra_ref, total_ref):
    wide = jnp.concatenate([site, site], axis=1)
    rows, columns = iota(wide.shape, 0), iota(wide.shape, 1)
    shift = ((rows >> 2) - (columns >> 4)) & 3
    swapped = jnp.where(shift == 0, wide, 0.0)
    for k in range(1, D):
        moved = pltpu.roll(pltpu.roll(wide, D * k, 0), wide.shape[1] - D2 * k, 1)
        swapped = jnp.where(shift == k, moved, swapped)
    wide = jnp.where(odd == 1, swapped, wide)
    half = D * D2
    high = wide.astype(BF16)
    low = (wide - high.astype(F32)).astype(BF16)
    parts = jnp.where(columns < half, high.astype(F32), low.astype(F32)).astype(BF16)
    index, entry = iota((TILE, D2), 0), iota((TILE, D2), 1)
    ket_rows = select(entry == ((index >> 4 & 12) | (index >> 2 & 3)))
    bra_rows = select(entry == ((index >> 2 & 12) | (index & 3)))
    ket = dot(ket_rows, parts).astype(BF16)
    bra = dot(bra_rows, parts).astype(BF16)
    ket_ref[...] = ket
    bra_ref[...] = bra
    total_ref[...] = jnp.zeros_like(total_ref)

    def add(t, carry):
        index, entry = iota((TILE, 4 * half), 0), iota((TILE, 4 * half), 1)
        ket_place = (index & 12) << 2 | (index >> 6) << 2
        bra_place = (index & 3) << 4 | (index >> 2 & 12)
        lanes = iota((8, 4 * half), 1)
        column = jnp.zeros(lanes.shape, F32)
        for s in range(S):
            column = jnp.where((lanes & 3) == s, operator_ref[0, s, t], column)
        high = column.astype(BF16).astype(F32)
        column = jnp.where(lanes < 2 * half, high, column - high)[:1]
        kets = jnp.where((entry & 60) == ket_place, column, 0.0).astype(BF16)
        bras = select((entry & 63) == bra_place + t)[:, : 2 * half]
        total_ref[...] += dot_nt(kets, jnp.concatenate([ket_ref[...]] * 2, axis=1)) * dot_nt(bras, bra_ref[...])
        return carry

    lax.fori_loop(0, S, add, 0)
    return total_ref[...].astype(BF16)


def wide(ref):
    return jnp.concatenate([ref[i] for i in range(ref.shape[0])], axis=1)


def kernel(
    n_rows,
    n_columns,
    kept_ref,
    operator_hbm,
    site_hbm,
    front_hbm,
    factor_hbm,
    arrived_ref,
    divisor_ref,
    operator_ref,
    site_ref,
    front_ref,
    factor_ref,
    planes_ref,
    turned_ref,
    sent_ref,
    left_ref,
    relay_ref,
    front_planes_ref,
    swap_ref,
    identity_ref,
    ket_ref,
    bra_ref,
    total_ref,
    doubled_ref,
    projected_ref,
    absorbed_ref,
    unscaled_ref,
    quad_ref,
    ring_ref,
    load_sem,
    ready_sem,
    left_send,
    left_recv,
    relay_send,
    relay_recv,
    front_send,
    front_recv,
    quad_send,
    quad_recv,
    ring_send,
    ring_recv,
):
    n_ring = n_columns // QUAD
    row, column = lax.axis_index("rows"), lax.axis_index("cols")
    odd = lax.rem(row, 2)
    partner = row + 1 - 2 * odd
    before = lax.rem(column + n_columns - 1, n_columns)
    behind = lax.rem(column + 1, n_columns)
    place, member = column // QUAD, lax.rem(column, QUAD)
    core = lax.rem(column, 2)

    def beside_x(to_row, to_column, up):
        low = to_row // (n_rows // 2)
        flip = low if up else 1 - low
        start = (to_column // QUAD) * QUAD
        high = lax.rem(to_column, QUAD) // 2
        high = high + flip * (1 - 2 * high)
        return to_row + (n_rows // 2) * (1 - 2 * low), start + 2 * high + 1

    def load(source, target, k):
        copy = pltpu.make_async_copy(source, target, load_sem.at[k])
        copy.start()
        return copy

    def load_factor(i):
        piece = pl.ds(pl.multiple_of(i * 2 * TILE, 2 * TILE), 2 * TILE)
        return pltpu.make_async_copy(
            factor_hbm.at[piece, :], factor_ref.at[piece, :], load_sem.at[3 + i]
        )

    for i in range(CHUNKS // 2):
        load_factor(i).start()
    load_site = load(site_hbm, site_ref, 1)
    load_operator = load(operator_hbm, operator_ref, 2)
    load_front = load(front_hbm, front_ref, 0)

    barrier = pltpu.get_barrier_semaphore()

    def greet(to_row, to_column):
        pl.semaphore_signal(barrier, inc=1, device_id=(to_row, to_column), device_id_type=MESH)

    def quad_column(k):
        return place * QUAD + lax.rem(member + k, QUAD)

    def ring_column(k):
        return lax.rem(place + k + n_ring, n_ring) * QUAD + member

    greet(row, before)
    greet(row, behind)
    greet(partner, column)
    for k in range(1, QUAD):
        greet(row, quad_column(k))

    def far_first(k):
        return lax.rem(n_ring // 2 + n_ring + (2 * lax.rem(k, 2) - 1) * ((k + 1) // 2), n_ring)

    for k in (1, 2):
        greet(partner, ring_column(k))
        greet(partner, ring_column(-k))
    greet(row, ring_column(2))
    greet(row, ring_column(-2))

    def tell(n):
        for k in (-2 - 2 * n, 2 + 2 * n):
            pl.semaphore_signal(
                ready_sem.at[n],
                inc=1,
                device_id=(row, ring_column(k)),
                device_id_type=MESH,
            )

    relay = beside_x(row, column, 0)
    served = beside_x(row, column, 1)
    served_target = served[0], lax.rem(served[1] + 1, n_columns)
    left_relay = beside_x(row, before, 0)

    @pl.when(core == 1)
    def _():
        greet(*served)

    @pl.when(core == 0)
    def _():
        greet(*left_relay)

    def chunk(ref, i):
        return ref.at[pl.ds(pl.multiple_of(i * TILE, TILE), TILE), :]

    def rows_of(i, size):
        return pl.ds(pl.multiple_of(i * size, size), size)

    def beside(ref, i):
        block = ref[rows_of(i, 2 * TILE), :]
        return jnp.concatenate([block[:TILE], block[TILE:]], axis=1)

    swap = swap_16()
    swap_ref[0], swap_ref[1] = swap[:, :X], swap[:, X:]
    identity_ref[...] = select(iota((X, X), 0) == iota((X, X), 1))

    def permute(i, carry):
        load_factor(i).wait()
        kept = (iota((TILE, 2 * X), 1) & (X - 1)) < kept_ref[0, 0]
        block = dot(wide(swap_ref), beside(factor_ref, i))
        block = jnp.where(kept, block, 0.0).astype(BF16)
        for k in range(2):
            lanes = slice(k * X, (k + 1) * X)
            for q in range(D2):
                start = pl.multiple_of(q * X + i * 2 * D2 + k * D2, D2)
                planes_ref[pl.ds(start, D2), :] = block[q * D2 : (q + 1) * D2, lanes]
        return carry

    lax.fori_loop(0, CHUNKS // 2, permute, 0)

    def turn(i, carry):
        for n in range(4):
            block = planes_ref[rows_of(4 * i + n, 2 * X), :]
            both = dot_nt(identity_ref[...], block).astype(BF16)
            for k in range(2):
                for j in range(CHUNKS):
                    start = pl.multiple_of(j * TILE + (8 * i + 2 * n + k) * D2, D2)
                    turned_ref[pl.ds(start, D2), :] = both[
                        j * D2 : (j + 1) * D2, k * X : (k + 1) * X
                    ]
        return carry

    lax.fori_loop(0, D2 // 8, turn, 0)

    def interleave(i):
        both = dot(wide(swap_ref), beside(turned_ref, i)).astype(BF16)
        for k in range(2):
            sent_ref[rows_of(2 * i + k, TILE), :] = both[:, k * X : (k + 1) * X]

    interleave(0)
    pl.semaphore_wait(barrier, 2 + 1 + (QUAD - 1) + 6 + 2 * core)
    tell(0)

    def left_copy(i):
        return pltpu.make_async_remote_copy(
            src_ref=chunk(sent_ref, i),
            dst_ref=chunk(left_ref, i),
            send_sem=left_send.at[i],
            recv_sem=left_recv.at[i],
            device_id=(row, behind),
            device_id_type=MESH,
        )

    def relay_copy(i):
        return pltpu.make_async_remote_copy(
            src_ref=chunk(sent_ref, i),
            dst_ref=chunk(relay_ref, (i - 3) // 2),
            send_sem=left_send.at[i],
            recv_sem=relay_recv.at[(i - 3) // 2],
            device_id=relay,
            device_id_type=MESH,
        )

    def onward_copy(i):
        return pltpu.make_async_remote_copy(
            src_ref=chunk(relay_ref, (i - 3) // 2),
            dst_ref=chunk(left_ref, i),
            send_sem=relay_send.at[(i - 3) // 2],
            recv_sem=left_recv.at[i],
            device_id=served_target,
            device_id_type=MESH,
        )

    def pass_on(i):
        relay_copy(i).wait_recv()
        onward_copy(i).start()

    def start_left(i, carry):
        left_copy(i).start()
        return carry

    left_copy(0).start()
    for i in range(1, CHUNKS // 2):
        interleave(i)

    @pl.when(core == 0)
    def _():
        lax.fori_loop(1, CHUNKS, start_left, 0)

    @pl.when(core == 1)
    def _():
        relay_copy(3).start()

    def permute_front(i, carry):
        for n in range(2):
            both = dot(wide(swap_ref), beside(front_ref, 2 * i + n)).astype(BF16)
            for k in range(2):
                for v in range(D2):
                    start = pl.multiple_of(v * X + (4 * i + 2 * n + k) * D2, D2)
                    front_planes_ref[pl.ds(start, D2), :] = both[
                        v * D2 : (v + 1) * D2, k * X : (k + 1) * X
                    ]
        return carry

    load_front.wait()
    lax.fori_loop(0, CHUNKS // 4, permute_front, 0)

    @pl.when(core == 1)
    def _():
        left_copy(1).start()
        relay_copy(5).start()

    load_site.wait()
    load_operator.wait()
    doubled = double_layer(site_ref[0], operator_ref, odd, ket_ref, bra_ref, total_ref)
    doubled_ref[0], doubled_ref[1] = doubled[:, :X], doubled[:, X:]

    @pl.when(core == 1)
    def _():
        left_copy(2).start()

    def front_copy(i):
        return pltpu.make_async_remote_copy(
            src_ref=chunk(unscaled_ref, i),
            dst_ref=chunk(arrived_ref, i),
            send_sem=front_send.at[i],
            recv_sem=front_recv.at[i],
            device_id=(partner, column),
            device_id_type=MESH,
        )

    def project(i):
        left = left_ref[rows_of(i, TILE), :]
        for v in range(0, D2, 2):
            pair = jnp.concatenate(
                [front_planes_ref[v * X : (v + 1) * X], front_planes_ref[(v + 1) * X : (v + 2) * X]],
                axis=1,
            )
            both = dot(left, pair).astype(BF16)
            for k in range(2):
                projected_ref[:, (v + k) * D2 : (v + k + 1) * D2, :] = both[
                    :, k * X : (k + 1) * X
                ].reshape(D2, D2, X)

    def absorb():
        for a in range(0, D2, 2):
            pair = jnp.concatenate([projected_ref[a], projected_ref[a + 1]], axis=1)
            both = dot(wide(doubled_ref), pair).astype(BF16)
            for k in range(2):
                for q in range(D2):
                    absorbed_ref[q, (a + k) * D2 : (a + k + 1) * D2] = both[
                        q * D2 : (q + 1) * D2, k * X : (k + 1) * X
                    ]

    def work(i, top):
        @pl.when(i < CHUNKS - 1)
        def _():
            left_copy(i + 1).wait_recv()

        @pl.when((core == 1) & (i < 2))
        def _():
            pass_on(2 * i + 3)
            left_copy(2 * i + 4).start()

        @pl.when((core == 1) & (i == 0))
        def _():
            relay_copy(7).start()

        @pl.when((core == 1) & (i == 3))
        def _():
            pass_on(7)

        @pl.when(i == 2)
        def _():
            pl.semaphore_wait(ready_sem.at[0], 2)
            tell(1)

        absorb()
        project(jnp.minimum(i + 1, CHUNKS - 1))
        result = dot(wide(absorbed_ref), planes_ref[...])
        unscaled_ref[rows_of(i, TILE), :] = result.astype(BF16)
        front_copy(i).start()
        return jnp.maximum(top, jnp.max(jnp.abs(result).reshape(TILE // 8, 8, X), axis=0))

    left_copy(0).wait_recv()
    project(0)
    top = lax.fori_loop(0, CHUNKS, work, jnp.zeros((8, X), F32))
    top = jnp.max(top, axis=0, keepdims=True).astype(BF16).astype(F32)

    def quad_copy(k):
        return pltpu.make_async_remote_copy(
            src_ref=quad_ref.at[member],
            dst_ref=quad_ref.at[member],
            send_sem=quad_send.at[k],
            recv_sem=quad_recv.at[member],
            device_id=(row, quad_column(k)),
            device_id_type=MESH,
        )

    def arrival(ref, sems, slot):
        return pltpu.make_async_remote_copy(
            src_ref=ref.at[slot],
            dst_ref=ref.at[slot],
            send_sem=sems.at[slot],
            recv_sem=sems.at[slot],
            device_id=(row, behind),
            device_id_type=MESH,
        )

    pl.semaphore_wait(ready_sem.at[1], 2)
    quad_ref[member] = top
    for k in range(1, QUAD):
        quad_copy(k).start()
    for k in range(1, QUAD):
        arrival(quad_ref, quad_recv, lax.rem(member + k, QUAD)).wait_recv()
    ring_ref[n_ring] = jnp.max(quad_ref[...], axis=0)

    def ring_copy(k):
        return pltpu.make_async_remote_copy(
            src_ref=ring_ref.at[n_ring],
            dst_ref=ring_ref.at[place],
            send_sem=ring_send.at[k],
            recv_sem=ring_recv.at[place],
            device_id=(partner, ring_column(k)),
            device_id_type=MESH,
        )

    def start_ring(k, carry):
        ring_copy(far_first(k)).start()
        return carry

    def end_ring(k, carry):
        arrival(ring_ref, ring_recv, lax.rem(place + k, n_ring)).wait_recv()
        ring_copy(k).wait_send()
        return carry

    lax.fori_loop(0, n_ring, start_ring, 0)
    lax.fori_loop(0, n_ring, end_ring, 0)
    largest = jnp.max(ring_ref[:n_ring], axis=0)
    divisor_ref[0, 0] = jnp.max(largest) + EPSILON

    for k in range(1, QUAD):
        quad_copy(k).wait_send()

    def finish(i, carry):
        left_copy(i).wait_send()
        front_copy(i).wait()
        return carry

    lax.fori_loop(0, CHUNKS, finish, 0)

    @pl.when(core == 1)
    def _():
        for i in range(3, CHUNKS, 2):
            onward_copy(i).wait_send()


def per_device(fronts, factors, site_tensors, operators, kept_ranks):
    n_rows, n_columns = lax.axis_size("rows"), lax.axis_size("cols")
    rows = X * D2
    smem = pl.BlockSpec(memory_space=pltpu.SMEM)
    hbm = pl.BlockSpec(memory_space=pltpu.HBM)
    anywhere = pl.BlockSpec(memory_space=pl.ANY)
    dma = pltpu.SemaphoreType.DMA

    def body(*refs):
        kernel(n_rows, n_columns, *refs)

    flops = 2 * 4 * X * X * X * D2 * D2
    arrived, divisor = pl.pallas_call(
        body,
        out_shape=(
            jax.ShapeDtypeStruct((rows, X), BF16),
            jax.ShapeDtypeStruct((1, 1), F32),
        ),
        in_specs=[smem] + [hbm] * 4,
        out_specs=(anywhere, smem),
        scratch_shapes=[
            pltpu.SMEM(operators.shape, F32),
            pltpu.VMEM(site_tensors.shape, F32),
            pltpu.VMEM((rows, X), BF16),
            pltpu.VMEM((rows, X), BF16),
            pltpu.VMEM((rows, X), BF16),
            pltpu.VMEM((rows, X), BF16),
            pltpu.VMEM((rows, X), BF16),
            pltpu.VMEM((rows, X), BF16),
            pltpu.VMEM((rows // 2, X), BF16),
            pltpu.VMEM((rows, X), BF16),
            pltpu.VMEM((2, TILE, X), BF16),
            pltpu.VMEM((X, X), BF16),
            pltpu.VMEM((TILE, X), BF16),
            pltpu.VMEM((TILE, X), BF16),
            pltpu.VMEM((TILE, TILE), F32),
            pltpu.VMEM((2, TILE, X), BF16),
            pltpu.VMEM((D2, TILE, X), BF16),
            pltpu.VMEM((D2, TILE, X), BF16),
            pltpu.VMEM((rows, X), BF16),
            pltpu.VMEM((QUAD, 1, X), F32),
            pltpu.VMEM((n_columns // QUAD + 1, 1, X), F32),
            dma((3 + CHUNKS // 2,)),
            pltpu.SemaphoreType.REGULAR((2,)),
            dma((CHUNKS,)),
            dma((CHUNKS,)),
            dma((CHUNKS // 2,)),
            dma((CHUNKS // 2,)),
            dma((CHUNKS,)),
            dma((CHUNKS,)),
            dma((QUAD,)),
            dma((QUAD,)),
            dma((n_columns // QUAD,)),
            dma((n_columns // QUAD,)),
        ],
        compiler_params=pltpu.CompilerParams(
            collective_id=0, has_side_effects=True, vmem_limit_bytes=40 * 2**20
        ),
        cost_estimate=pl.CostEstimate(flops=flops, bytes_accessed=3 * 2**19, transcendentals=0),
    )(
        kept_ranks,
        *(
            pltpu.with_memory_space_constraint(operand, pltpu.HBM)
            for operand in (
                operators,
                site_tensors,
                fronts.reshape(rows, X),
                factors.reshape(rows, X),
            )
        )
    )
    normalized = arrived.astype(F32) / divisor[0, 0]
    return normalized.astype(BF16).reshape(1, X, D2, X)


def solution(mesh):
    return jax.shard_map(
        per_device,
        mesh=mesh,
        in_specs=(
            P("rows", None, None, "cols"),
            P("rows", None, "cols"),
            P("rows", None, "cols"),
            P("rows", None, "cols"),
            P("rows", "cols"),
        ),
        out_specs=P("rows", None, None, "cols"),
        check_vma=False,
    )
```
